128 devices in a mesh: img: 4 (over x), pix: 32 (over z, y, core).
Axes of the slice: x: 4, y: 4, z: 4, core: 2. Of those that a mesh axis runs over, the one named last changes fastest.
Arguments:
- step_ids: int32 [16], replicated, may hold values from 0 to 1023, as said below
- grid_table: float32 [1024, 12, 2048], P(('img', 'pix'))
- tile_image: int32 [2048], P(('img', 'pix')), may hold values from 0 to 3
- cell_index: int32 [2097152], P(('img', 'pix')), may hold values from 0 to 1910, as said below
- fractions: float32 [3, 2097152], P(None, ('img', 'pix')), may hold values from 0 to 1
- features: bfloat16 [64, 2097152], P(None, ('img', 'pix')), may hold values from -6 to 6
- head_weight: bfloat16 [3, 64], replicated, may hold values from -0.75 to 0.75
- head_bias: float32 [3], replicated, may hold values from -3 to 3
- cotangent: bfloat16 [3, 2097152], P(None, ('img', 'pix')), may hold values from -1.5 to 1.5
Outputs:
- owned_grads: float32 [256, 12, 2048], P(('img', 'pix'))
- head_grad: float32 [3, 64], replicated
- bias_grad: float32 [3], replicated
- feature_grad: bfloat16 [64, 2097152], P(None, ('img', 'pix'))
The draws below stay inside these ranges and needn't reach their ends.
Inputs may be any that keep to these rules, and one draw needn't show every extreme that they name: `step_ids`: distinct; the holder step_ids // 8 has at most 2 of them, and some holder has exactly 2. `cell_index`: every corner cell stays inside the grid.
All inputs are finite; a program needn't handle non-finite values.
Results may differ from the reference program's by a relative error of at most 0.0049.
Values sent between devices are 32-bit elements; how exact they have to be, the bound alone decides.
A program may use at most 64 MiB of HBM per device.

```python
import math
import jax
import jax.numpy as jnp
import numpy as np
from jax import lax

GX = 16
GY = 16
GZ = 8
FEAT = 64
TILE = 1024
TILES_DEV = 16
IMG_ROW = 4
TAB_DEV = 8
OWN_MOST = 2
CELLS = 2048
IMG_STEP = 16
NTAB = 1024
TILES = 2048
PIXELS = 2097152
N_PIX = 32
DEVICES = 128


def draw_step_ids(key, part):
    key = jax.random.fold_in(key, 11)
    key_owner, key_rows, key_order = jax.random.split(key, 3)
    others = jax.random.permutation(key_owner, DEVICES - 1).astype(jnp.int32)
    last_dev = jnp.array([DEVICES - 1], jnp.int32)
    holders = jnp.concatenate([last_dev, others[:IMG_STEP - 2], last_dev])
    first_rows = jax.random.randint(key_rows, (IMG_STEP - 1,), 0, TAB_DEV // 2).astype(jnp.int32)
    table_rows = jnp.concatenate([first_rows, jnp.array([TAB_DEV - 1], jnp.int32)])
    identities = holders * TAB_DEV + table_rows
    shuffle = jax.random.permutation(key_order, IMG_STEP)
    return identities[shuffle].astype(jnp.int32)


def draw_grid_table(key, part):
    key = jax.random.fold_in(key, 23)
    coefs = jnp.arange(12)
    identity = (coefs // 4 == coefs % 4).astype(jnp.float32)[None, :, None]
    noise = 0.15 * jax.random.normal(key, (NTAB, 12, CELLS), jnp.float32)
    return (identity + noise).astype(jnp.float32)


def draw_cell_index(key, part):
    key = jax.random.fold_in(key, 37)
    key_x, key_y, key_z = jax.random.split(key, 3)
    coord_x = jax.random.randint(key_x, (PIXELS,), 0, GX - 1)
    coord_y = jax.random.randint(key_y, (PIXELS,), 0, GY - 1)
    coord_z = jax.random.randint(key_z, (PIXELS,), 0, GZ - 1)
    flat = (coord_x * GY + coord_y) * GZ + coord_z
    top_cell = (GX - 2) * GY * GZ + (GY - 2) * GZ + GZ - 2
    flat = flat.at[0].set(top_cell).at[1].set(0)
    return flat.astype(jnp.int32)


def plant(values, rng, low, top_value):
    spot = [jax.random.randint(jax.random.fold_in(rng, axis), (), 0, length) for axis, length in enumerate(values.shape)]
    widest = values.shape.index(max(values.shape))
    neighbour = spot[:widest] + [(spot[widest] + 1) % values.shape[widest]] + spot[widest + 1:]
    return values.at[tuple(spot)].set(low).at[tuple(neighbour)].set(top_value)


def block_scale(stream_key, dims, cuts, low, largest):
    loudness, own = 1.0, jax.random.fold_in(stream_key, 6)
    for dim, shards_of in cuts:
        heights = jnp.exp(jax.random.uniform(jax.random.fold_in(own, dim), (shards_of,), jnp.float32, low / len(cuts), largest / len(cuts)))
        loudness = loudness * jnp.repeat(heights, dims[dim] // shards_of).reshape([-1 if axis == dim else 1 for axis in range(len(dims))])
    return loudness


def rank_table(amount, slope):
    portions = [(1 << 20) // math.isqrt(rank ** slope) + 1 for rank in range(1, amount + 1)]
    scale = 1 + sum(portions) // (1 << 30)
    return np.cumsum(np.array([max(1, weight // scale) for weight in portions]))


def ranked(key, extent, amount, lean):
    listing = rank_table(amount, lean)
    ticket = jax.random.randint(jax.random.fold_in(key, 1), extent, 0, int(listing[amount - 1]))
    grade = jnp.searchsorted(jnp.asarray(listing, jnp.int32), ticket, side="right")
    return jax.random.permutation(jax.random.fold_in(key, 2), amount)[grade].astype(jnp.int32)


def gaussian(own_key, extent, width, most, cuts=(), kind=jnp.bfloat16):
    factor_of = block_scale(own_key, extent, cuts, -0.22, 0.18) if cuts else 1.0
    values = jax.random.normal(own_key, extent, jnp.float32) * width * factor_of
    return jnp.minimum(jnp.maximum(values, -most), most).astype(kind)


def setup_inputs(seed: int = 0) -> dict:
    arg_keys = jax.random.split(jax.random.key(seed), 10)
    return {
        "step_ids": draw_step_ids(jax.random.fold_in(arg_keys[9], 71), 0),
        "grid_table": draw_grid_table(jax.random.fold_in(arg_keys[9], 71), 0),
        "tile_image": plant(ranked(arg_keys[2], (TILES,), IMG_ROW, 2), jax.random.fold_in(arg_keys[2], 3), 0, IMG_ROW - 1).astype(jnp.int32),
        "cell_index": draw_cell_index(jax.random.fold_in(arg_keys[9], 71), 0),
        "fractions": jnp.clip(1.0 * jax.random.uniform(arg_keys[4], (3, PIXELS), jnp.float32) ** block_scale(arg_keys[4], (3, PIXELS), ((1, 128),), -0.2, 0.2), 0.0, 1.0),
        "features": gaussian(arg_keys[5], (FEAT, PIXELS), 1.0, 6.0, ((1, 128),)),
        "head_weight": gaussian(arg_keys[6], (3, FEAT), FEAT ** -0.5, 0.75),
        "head_bias": gaussian(arg_keys[7], (3,), 1.0, 3.0, (), jnp.float32),
        "cotangent": gaussian(arg_keys[8], (3, PIXELS), 0.2, 1.5, ((1, 128),)),
    }


def corner_list(cell_index, fractions):
    result = []
    for dx in (0, 1):
        for dy in (0, 1):
            for dz in (0, 1):
                wx = fractions[0] if dx else 1.0 - fractions[0]
                wy = fractions[1] if dy else 1.0 - fractions[1]
                wz = fractions[2] if dz else 1.0 - fractions[2]
                offset = dx * GY * GZ + dy * GZ + dz
                result.append((cell_index + offset, wx * wy * wz))
    return result


def tv_gradient(grids):
    shaped = grids.reshape(grids.shape[0], 12, GX, GY, GZ)
    summed = jnp.zeros_like(shaped)
    for axis in (2, 3, 4):
        diffs = jnp.diff(shaped, axis=axis)
        zero_shape = list(diffs.shape)
        zero_shape[axis] = 1
        zeros_rim = jnp.zeros(zero_shape, jnp.float32)
        summed = summed + (jnp.concatenate([zeros_rim, diffs], axis=axis) - jnp.concatenate([diffs, zeros_rim], axis=axis))
    return (2.0 * 0.5 * summed).reshape(grids.shape)


def reference(step_ids, grid_table, tile_image, cell_index, fractions, features, head_weight, head_bias, cotangent):
    step_grids = grid_table[step_ids]
    tile_rows = jnp.arange(TILES, dtype=jnp.int32) // (TILES_DEV * N_PIX)
    image_tile = tile_rows * IMG_ROW + tile_image
    image_of = jnp.repeat(image_tile, TILE)
    logits = jnp.dot(head_weight, features, preferred_element_type=jnp.float32) + head_bias[:, None]
    colour = jax.nn.sigmoid(logits)
    upstream = cotangent.astype(jnp.float32)
    flat_grids = jnp.transpose(step_grids, (1, 0, 2)).reshape(12, IMG_STEP * CELLS)
    corners = corner_list(cell_index, fractions)
    coeffs = None
    for corner_idx, weights in corners:
        term = weights[None, :] * flat_grids[:, image_of * CELLS + corner_idx]
        coeffs = term if coeffs is None else coeffs + term
    inputs = jnp.concatenate([colour, jnp.ones((1, PIXELS), jnp.float32)], axis=0)
    d_coeffs = (upstream[:, None, :] * inputs[None, :, :]).reshape(12, PIXELS)
    d_colour = (coeffs[0:3] * upstream[0] + coeffs[4:7] * upstream[1]) + coeffs[8:11] * upstream[2]
    d_logits = d_colour * colour * (1.0 - colour)
    d_half = d_logits.astype(jnp.bfloat16)
    feature_grad = lax.dot_general(head_weight, d_half, (((0,), (0,)), ((), ())), preferred_element_type=jnp.float32).astype(jnp.bfloat16)
    head_grad = lax.dot_general(d_half, features, (((1,), (1,)), ((), ())), preferred_element_type=jnp.float32)
    bias_grad = jnp.sum(d_logits, axis=1)
    flat_grads = jnp.zeros((12, IMG_STEP * CELLS), jnp.float32)
    for corner_idx, weights in corners:
        flat_grads = flat_grads.at[:, image_of * CELLS + corner_idx].add(weights[None, :] * d_coeffs)
    data_grads = jnp.transpose(flat_grads.reshape(12, IMG_STEP, CELLS), (1, 0, 2))
    step_total = data_grads + tv_gradient(step_grids)
    holders = step_ids // TAB_DEV
    positions = jnp.arange(IMG_STEP, dtype=jnp.int32)
    earlier = (positions[None, :] < positions[:, None]) & (holders[None, :] == holders[:, None])
    order_rank = jnp.sum(earlier.astype(jnp.int32), axis=1)
    slots = holders * OWN_MOST + order_rank
    owned_grads = jnp.zeros((DEVICES * OWN_MOST, 12, CELLS), jnp.float32).at[slots].set(step_total)
    return owned_grads, head_grad, bias_grad, feature_grad
```

```python
import functools

import jax
import jax.numpy as jnp
from jax import lax
from jax.experimental import pallas as pl
from jax.experimental.pallas import tpu as pltpu
from jax.sharding import PartitionSpec as P

GX = 16
GY = 16
GZ = 8
YZ = GY * GZ
CELLS = GX * YZ
COEF = 12
TILE = 1024
IMG_ROW = 4
OWN_MOST = 2
ROWS = COEF * GX
USED = 9 * GX
MESH = pl.DeviceIdType.MESH
NT = (((1,), (1,)), ((), ()))


def spread(block):
    return jnp.concatenate(
        [jnp.broadcast_to(block[s : s + 1, :], (8, 128)) for s in range(8)], axis=1
    )


def hat(coord, level, low, high):
    return jnp.where(coord == level, low, jnp.where(coord == level - 1, high, 0.0))


def kernel(
    planes,
    rows_x,
    ids_ref,
    tile_ref,
    bias_ref,
    table_ref,
    cell_ref,
    frac_ref,
    feat_ref,
    weight_ref,
    cot_ref,
    owned_ref,
    head_ref,
    fgrad_ref,
    splat_ref,
    uax_ref,
    colour_ref,
    acc_ref,
    sib_ref,
    total_ref,
    grid_f32,
    grid_ref,
    tv_ref,
    stat_ref,
    head_acc,
    bias_acc,
    holder_q,
    holder_g,
    rank_ref,
    dest_ref,
    g1_send,
    g1_recv,
    g2_send,
    g2_recv,
    g3_send,
    g3_recv,
    r1_send,
    r1_recv,
    r2_send,
    r2_recv,
    r3_send,
    r3_recv,
    h1_recv,
    h2_send,
    h2_recv,
    sib_sems,
    plane_ss,
    plane_rs,
    line_ss,
    line_rs,
):
    tiles = cell_ref.shape[0] // 8
    images = ids_ref.shape[0]
    groups = rows_x * 2
    my_x = lax.axis_index("img")
    my_pix = lax.axis_index("pix")
    my_q = my_pix // 2
    my_c = my_pix % 2
    my_g = my_x * 2 + my_c
    my_dev = my_x * (planes * 2) + my_pix

    def plane_copy(stage, q, src, dst):
        return pltpu.make_async_remote_copy(
            src_ref=src,
            dst_ref=dst,
            send_sem=plane_ss.at[stage, q],
            recv_sem=plane_rs.at[stage, my_q],
            device_id={"img": my_x, "pix": q * 2 + my_c},
            device_id_type=MESH,
        )

    def line_copy(stage, g, src, dst):
        return pltpu.make_async_remote_copy(
            src_ref=src,
            dst_ref=dst,
            send_sem=line_ss.at[stage, g],
            recv_sem=line_rs.at[stage, my_g],
            device_id={"img": g // 2, "pix": my_q * 2 + g % 2},
            device_id_type=MESH,
        )

    def plane_each(fn):
        def step(o, carry):
            fn((my_q + o) % planes)
            return carry

        lax.fori_loop(1, planes, step, 0)

    def line_each(fn):
        def step(o, carry):
            fn((my_g + o) % groups)
            return carry

        lax.fori_loop(1, groups, step, 0)

    def plane_arrive(stage, buf):
        def one(q):
            pltpu.make_async_remote_copy(
                src_ref=buf.at[q],
                dst_ref=buf.at[q],
                send_sem=plane_ss.at[stage, q],
                recv_sem=plane_rs.at[stage, q],
                device_id={"img": my_x, "pix": q * 2 + my_c},
                device_id_type=MESH,
            ).wait_recv()

        plane_each(one)

    def line_arrive(stage, buf):
        def one(g):
            pltpu.make_async_remote_copy(
                src_ref=buf.at[g],
                dst_ref=buf.at[g],
                send_sem=line_ss.at[stage, g],
                recv_sem=line_rs.at[stage, g],
                device_id={"img": g // 2, "pix": my_q * 2 + g % 2},
                device_id_type=MESH,
            ).wait_recv()

        line_each(one)

    barrier = pltpu.get_barrier_semaphore()

    def greet_plane(q):
        pl.semaphore_signal(
            barrier,
            inc=1,
            device_id={"img": my_x, "pix": q * 2 + my_c},
            device_id_type=MESH,
        )

    def greet_line(g):
        pl.semaphore_signal(
            barrier,
            inc=1,
            device_id={"img": g // 2, "pix": my_q * 2 + g % 2},
            device_id_type=MESH,
        )

    plane_each(greet_plane)
    line_each(greet_line)

    holders = []
    ranks = []
    for i in range(images):
        holder = ids_ref[i] // table_ref.shape[0]
        rank = jnp.int32(0)
        for other in holders:
            rank = rank + jnp.where(other == holder, 1, 0)
        holders.append(holder)
        ranks.append(rank)
        hx = holder // (planes * 2)
        hp = holder % (planes * 2)
        holder_q[i] = hp // 2
        holder_g[i] = hx * 2 + hp % 2
        rank_ref[i] = jnp.minimum(rank, OWN_MOST - 1)

    own_row = [jnp.int32(0)] * OWN_MOST
    own_has = [jnp.int32(0)] * OWN_MOST
    for i in range(images):
        for s in range(OWN_MOST):
            hit = (holders[i] == my_dev) & (ranks[i] == s)
            own_row[s] = jnp.where(hit, ids_ref[i] % table_ref.shape[0], own_row[s])
            own_has[s] = jnp.where(hit, 1, own_has[s])

    for s in range(OWN_MOST):
        for q in range(planes):
            g1_send[q, s] = table_ref[own_row[s], :, q * YZ : (q + 1) * YZ]

    pl.semaphore_wait(barrier, planes - 1 + groups - 1)
    plane_each(lambda q: plane_copy(0, q, g1_send.at[q], g1_recv.at[my_q]).start())
    g1_recv[my_q] = g1_send[my_q]

    def find_dest(q, carry):
        dev = my_x * (planes * 2) + q * 2 + my_c
        for s in range(OWN_MOST):
            found = jnp.int32(images)
            for i in range(images):
                found = jnp.where((holders[i] == dev) & (ranks[i] == s), i, found)
            dest_ref[q * OWN_MOST + s] = found
        return carry

    lax.fori_loop(0, planes, find_dest, 0)

    lane = lax.broadcasted_iota(jnp.int32, (COEF, YZ), 1)
    for s in range(OWN_MOST):
        for q in range(planes):
            here = g1_send[q, s]
            total = jnp.zeros((COEF, YZ), jnp.float32)
            if q > 0:
                total = total + (here - g1_send[q - 1, s])
            if q < planes - 1:
                total = total - (g1_send[q + 1, s] - here)
            for step, first, last in (
                (GZ, lane >= GZ, lane < YZ - GZ),
                (1, lane % GZ != 0, lane % GZ != GZ - 1),
            ):
                before = jnp.where(first, here - pltpu.roll(here, step, 1), 0.0)
                after = jnp.where(last, pltpu.roll(here, YZ - step, 1) - here, 0.0)
                total = total + (before - after)
            tv_ref[s, :, q * YZ : (q + 1) * YZ] = jnp.where(own_has[s] == 1, total, 0.0)

    acc_ref[...] = jnp.zeros_like(acc_ref)
    head_acc[...] = jnp.zeros_like(head_acc)
    bias_acc[...] = jnp.zeros_like(bias_acc)

    def gather_two():
        plane_arrive(0, g1_recv)
        for i in range(images):
            g2_send[i // IMG_ROW, i % IMG_ROW] = g1_recv[holder_q[i], rank_ref[i]]
        line_each(
            lambda g: line_copy(0, g, g2_send.at[g // 2], g2_recv.at[my_g]).start()
        )
        g2_recv[my_g] = g2_send[my_x]

    def gather_three():
        line_arrive(0, g2_recv)
        for i in range(IMG_ROW):
            g3_send[i] = g2_recv[holder_g[my_x * IMG_ROW + i], i]
        plane_each(lambda q: plane_copy(1, q, g3_send, g3_recv.at[my_q]).start())
        g3_recv[my_q] = g3_send[...]

    def splat_tile(t, carry):
        @pl.when(t == tiles // 4)
        def _():
            gather_two()

        @pl.when(t == tiles // 2)
        def _():
            gather_three()

        px = pl.ds(pl.multiple_of(t * TILE, TILE), TILE)
        cell = spread(cell_ref[pl.ds(pl.multiple_of(t * 8, 8), 8), :])
        cx = cell // YZ
        cy = (cell // GZ) % GY
        cz = cell % GZ
        fx = jnp.broadcast_to(frac_ref[0:1, px], (8, TILE))
        fy = jnp.broadcast_to(frac_ref[1:2, px], (8, TILE))
        fz = jnp.broadcast_to(frac_ref[2:3, px], (8, TILE))
        low_level = lax.broadcasted_iota(jnp.int32, (8, TILE), 0)
        az = hat(cz, low_level, 1.0 - fz, fz)
        gy = 1.0 - fy
        for y in range(0, GY, 2):
            pair = jnp.concatenate(
                [hat(cy, y, gy, fy) * az, hat(cy, y + 1, gy, fy) * az], axis=0
            )
            big = pair.astype(jnp.bfloat16)
            rest = (pair - big.astype(jnp.float32)).astype(jnp.bfloat16)
            splat_ref[t, y * GZ : (y + 2) * GZ, :] = big
            splat_ref[t, YZ + y * GZ : YZ + (y + 2) * GZ, :] = rest
        gx = 1.0 - fx
        ax = jnp.concatenate(
            [hat(cx, low_level, gx, fx), hat(cx, low_level + 8, gx, fx)], axis=0
        )
        logits = jnp.dot(
            weight_ref[...], feat_ref[:, px], preferred_element_type=jnp.float32
        )
        chan = lax.broadcasted_iota(jnp.int32, (3, TILE), 0)
        bias = jnp.where(
            chan == 0, bias_ref[0], jnp.where(chan == 1, bias_ref[1], bias_ref[2])
        )
        colour = 1.0 / (1.0 + jnp.exp(-(logits + bias)))
        colour_ref[t, 0:3, :] = colour
        parts = []
        for k in range(3):
            u = jnp.broadcast_to(cot_ref[k : k + 1, px].astype(jnp.float32), (GX, TILE))
            uax = u * ax
            uax_ref[t, k * GX : (k + 1) * GX, :] = uax
            for j in range(3):
                col = jnp.broadcast_to(colour[j : j + 1, :], (GX, TILE))
                parts.append((uax * col).astype(jnp.bfloat16))
            parts.append(uax.astype(jnp.bfloat16))
        left = jnp.concatenate(parts, axis=0)
        both = lax.dot_general(
            left, splat_ref[t], NT, preferred_element_type=jnp.float32
        )
        grads = both[:, :YZ] + both[:, YZ:]
        image = tile_ref[t]
        for i in range(IMG_ROW):
            acc_ref[i] += jnp.where(image == i, grads, 0.0)
        return carry

    lax.fori_loop(0, tiles, splat_tile, 0)

    sibling = pltpu.make_async_remote_copy(
        src_ref=acc_ref.at[pl.ds(2 * (1 - my_c), 2)],
        dst_ref=sib_ref,
        send_sem=sib_sems.at[0],
        recv_sem=sib_sems.at[1],
        device_id={"img": my_x, "pix": my_q * 2 + 1 - my_c},
        device_id_type=MESH,
    )
    sibling.start()

    plane_arrive(1, g3_recv)
    for i in range(IMG_ROW):
        for q in range(planes):
            grid_f32[i, pl.ds(q, COEF, stride=GX), :] = g3_recv[q, i]
    for i in range(IMG_ROW):
        full = jnp.concatenate(
            [grid_f32[i, 4 * k * GX : (4 * k + 3) * GX, :] for k in range(3)], axis=0
        )
        big = full.astype(jnp.bfloat16)
        rest = (full - big.astype(jnp.float32)).astype(jnp.bfloat16)
        grid_ref[i, 0:USED, 0:YZ] = big
        grid_ref[i, 0:USED, YZ : 2 * YZ] = big
        grid_ref[i, USED : 2 * USED, 0:YZ] = rest
        grid_ref[i, USED : 2 * USED, YZ : 2 * YZ] = rest

    sibling.wait()
    for i in range(2):
        total_ref[i] = acc_ref[2 * my_c + i] + sib_ref[i]
    for q in range(planes):
        for i in range(2):
            r1_send[q, i] = total_ref[i, pl.ds(q, COEF, stride=GX), :]
    plane_each(lambda q: plane_copy(2, q, r1_send.at[q], r1_recv.at[my_q]).start())
    r1_recv[my_q] = r1_send[my_q]

    def reduce_two():
        plane_arrive(2, r1_recv)
        for i in range(2):
            total = r1_recv[0, i]
            for q in range(1, planes):
                total = total + r1_recv[q, i]
            r2_send[i] = total
        line_each(lambda g: line_copy(1, g, r2_send, r2_recv.at[my_g]).start())
        r2_recv[my_g] = r2_send[...]
        r2_recv[groups] = jnp.zeros_like(r2_send)

    def reduce_three():
        line_arrive(1, r2_recv)
        for q in range(planes):
            for s in range(OWN_MOST):
                i = dest_ref[q * OWN_MOST + s]
                r3_send[q, s] = r2_recv[i // 2, i % 2]
        plane_each(lambda q: plane_copy(3, q, r3_send.at[q], r3_recv.at[my_q]).start())
        r3_recv[my_q] = r3_send[my_q]

    weight_t = weight_ref[...].astype(jnp.float32).T.astype(jnp.bfloat16)

    def slice_tile(t, carry):
        @pl.when(t == tiles // 2)
        def _():
            reduce_two()

        @pl.when(t == tiles - tiles // 4)
        def _():
            reduce_three()

        px = pl.ds(pl.multiple_of(t * TILE, TILE), TILE)
        wide = jnp.dot(
            grid_ref[tile_ref[t]], splat_ref[t], preferred_element_type=jnp.float32
        )
        sums = []
        for j in range(3):
            total = None
            for k in range(3):
                at = (3 * k + j) * GX
                coef = wide[at : at + GX] + wide[USED + at : USED + at + GX]
                term = coef * uax_ref[t, k * GX : (k + 1) * GX, :]
                total = term if total is None else total + term
            sums.append(jnp.sum(total, axis=0, keepdims=True))
        d_colour = jnp.concatenate(sums, axis=0)
        colour = colour_ref[t, 0:3, :]
        d_logits = d_colour * colour * (1.0 - colour)
        d_half = d_logits.astype(jnp.bfloat16)
        fgrad_ref[:, px] = jnp.dot(
            weight_t, d_half, preferred_element_type=jnp.float32
        ).astype(jnp.bfloat16)
        head_acc[...] += lax.dot_general(
            d_half, feat_ref[:, px], NT, preferred_element_type=jnp.float32
        )
        bias_acc[...] += d_logits
        return carry

    lax.fori_loop(0, tiles, slice_tile, 0)

    bias_sum = jnp.sum(bias_acc[...], axis=1, keepdims=True)
    stat_ref[...] = jnp.zeros_like(stat_ref)
    stat_ref[0:3, :] = jnp.concatenate(
        [head_acc[...], jnp.broadcast_to(bias_sum, head_acc.shape)], axis=1
    )
    plane_each(lambda q: plane_copy(4, q, stat_ref, h1_recv.at[my_q]).start())
    h1_recv[my_q] = stat_ref[...]
    plane_arrive(3, r3_recv)
    for s in range(OWN_MOST):
        for q in range(planes):
            cols = slice(q * YZ, (q + 1) * YZ)
            owned_ref[s, :, cols] = r3_recv[q, s] + tv_ref[s, :, cols]
    plane_arrive(4, h1_recv)
    total = h1_recv[0]
    for q in range(1, planes):
        total = total + h1_recv[q]
    h2_send[...] = total
    line_each(lambda g: line_copy(2, g, h2_send, h2_recv.at[my_g]).start())
    h2_recv[my_g] = total
    line_arrive(2, h2_recv)
    total = h2_recv[0]
    for g in range(1, groups):
        total = total + h2_recv[g]
    head_ref[...] = total

    def plane_sent(q):
        plane_copy(0, q, g1_send.at[q], g1_recv.at[my_q]).wait_send()
        plane_copy(1, q, g3_send, g3_recv.at[my_q]).wait_send()
        plane_copy(2, q, r1_send.at[q], r1_recv.at[my_q]).wait_send()
        plane_copy(3, q, r3_send.at[q], r3_recv.at[my_q]).wait_send()
        plane_copy(4, q, stat_ref, h1_recv.at[my_q]).wait_send()

    def line_sent(g):
        line_copy(0, g, g2_send.at[g // 2], g2_recv.at[my_g]).wait_send()
        line_copy(1, g, r2_send, r2_recv.at[my_g]).wait_send()
        line_copy(2, g, h2_send, h2_recv.at[my_g]).wait_send()

    plane_each(plane_sent)
    line_each(line_sent)


def shards(planes, rows_x, ids, table, tile_image, cell, frac, feat, weight, bias, cot):
    pixels = cell.shape[0]
    tiles = pixels // TILE
    groups = rows_x * 2
    images = ids.shape[0]
    f32, bf16 = jnp.float32, jnp.bfloat16
    chunk = (COEF, YZ)
    vmem = pl.BlockSpec(memory_space=pltpu.VMEM)
    smem = pl.BlockSpec(memory_space=pltpu.SMEM)
    owned, head, fgrad = pl.pallas_call(
        functools.partial(kernel, planes, rows_x),
        out_shape=(
            jax.ShapeDtypeStruct((OWN_MOST, COEF, CELLS), f32),
            jax.ShapeDtypeStruct((8, 128), f32),
            jax.ShapeDtypeStruct(feat.shape, bf16),
        ),
        in_specs=[smem, smem, smem] + [vmem] * 6,
        out_specs=(vmem, vmem, vmem),
        scratch_shapes=[
            pltpu.VMEM((tiles, 2 * YZ, TILE), bf16),
            pltpu.VMEM((tiles, 3 * GX, TILE), f32),
            pltpu.VMEM((tiles, 8, TILE), f32),
            pltpu.VMEM((IMG_ROW, ROWS, YZ), f32),
            pltpu.VMEM((2, ROWS, YZ), f32),
            pltpu.VMEM((2, ROWS, YZ), f32),
            pltpu.VMEM((IMG_ROW, ROWS, YZ), f32),
            pltpu.VMEM((IMG_ROW, 2 * USED, 2 * YZ), bf16),
            pltpu.VMEM((OWN_MOST, COEF, CELLS), f32),
            pltpu.VMEM((8, 128), f32),
            pltpu.VMEM((3, feat.shape[0]), f32),
            pltpu.VMEM((3, TILE), f32),
            pltpu.SMEM((images,), jnp.int32),
            pltpu.SMEM((images,), jnp.int32),
            pltpu.SMEM((images,), jnp.int32),
            pltpu.SMEM((planes * OWN_MOST,), jnp.int32),
            pltpu.VMEM((planes, OWN_MOST) + chunk, f32),
            pltpu.VMEM((planes, OWN_MOST) + chunk, f32),
            pltpu.VMEM((rows_x, IMG_ROW) + chunk, f32),
            pltpu.VMEM((groups, IMG_ROW) + chunk, f32),
            pltpu.VMEM((IMG_ROW,) + chunk, f32),
            pltpu.VMEM((planes, IMG_ROW) + chunk, f32),
            pltpu.VMEM((planes, 2) + chunk, f32),
            pltpu.VMEM((planes, 2) + chunk, f32),
            pltpu.VMEM((2,) + chunk, f32),
            pltpu.VMEM((groups + 1, 2) + chunk, f32),
            pltpu.VMEM((planes, OWN_MOST) + chunk, f32),
            pltpu.VMEM((planes, OWN_MOST) + chunk, f32),
            pltpu.VMEM((planes, 8, 128), f32),
            pltpu.VMEM((8, 128), f32),
            pltpu.VMEM((groups, 8, 128), f32),
            pltpu.SemaphoreType.DMA((2,)),
            pltpu.SemaphoreType.DMA((5, planes)),
            pltpu.SemaphoreType.DMA((5, planes)),
            pltpu.SemaphoreType.DMA((3, groups)),
            pltpu.SemaphoreType.DMA((3, groups)),
        ],
        compiler_params=pltpu.CompilerParams(
            collective_id=0, has_side_effects=True, vmem_limit_bytes=48 << 20
        ),
    )(
        ids,
        tile_image,
        bias,
        table,
        cell.reshape(pixels // 128, 128),
        frac,
        feat,
        weight,
        cot,
    )
    return owned, head[0:3, 0 : feat.shape[0]], head[0:3, feat.shape[0]], fgrad


def solution(mesh):
    rows_x = mesh.shape["img"]
    planes = mesh.shape["pix"] // 2
    return jax.shard_map(
        functools.partial(shards, planes, rows_x),
        mesh=mesh,
        in_specs=(
            P(),
            P(("img", "pix"), None, None),
            P(("img", "pix")),
            P(("img", "pix")),
            P(None, ("img", "pix")),
            P(None, ("img", "pix")),
            P(),
            P(),
            P(None, ("img", "pix")),
        ),
        out_specs=(P(("img", "pix"), None, None), P(), P(), P(None, ("img", "pix"))),
        check_vma=False,
    )
```

```python
import functools
import math

import jax
import jax.numpy as jnp
from jax import lax
from jax.experimental import pallas as pl
from jax.experimental.pallas import tpu as pltpu
from jax.sharding import PartitionSpec as P

GX = 16
GY = 16
GZ = 8
YZ = GY * GZ
CELLS = GX * YZ
COEF = 12
TILE = 1024
IMG_ROW = 4
OWN_MOST = 2
ROWS = COEF * GX
USED = 9 * GX
VMEM_LIMIT = 40 << 20
SPLAT_FIRST = 10
SLICE_FIRST = 4
SLICE_SECOND = 12
MESH = pl.DeviceIdType.MESH
NT = (((1,), (1,)), ((), ()))


def spread(block):
    return jnp.concatenate(
        [jnp.broadcast_to(block[s : s + 1, :], (8, 128)) for s in range(8)], axis=1
    )


def hat(coord, level, low, high):
    return jnp.where(coord == level, low, jnp.where(coord == level - 1, high, 0.0))


def hops(a, b):
    return min(a % b, -a % b)


def kernel(
    side,
    rows_x,
    ids_any,
    tile_any,
    bias_any,
    table_any,
    cell_any,
    frac_any,
    feat_any,
    weight_any,
    cot_any,
    owned_ref,
    head_ref,
    fgrad_ref,
    ids_ref,
    tile_ref,
    bias_ref,
    table_ref,
    cell_ref,
    frac_ref,
    feat_ref,
    weight_ref,
    cot_ref,
    in_sems,
    splat_ref,
    uax_ref,
    colour_ref,
    half_ref,
    acc_ref,
    sib_ref,
    total_ref,
    grid_f32,
    grid_ref,
    tv_ref,
    stat_ref,
    head_acc,
    bias_acc,
    holder_q,
    holder_g,
    rank_ref,
    dest_ref,
    g1_send,
    g1_recv,
    g2_send,
    g2_recv,
    g3_send,
    g3_recv,
    r1_send,
    r1_recv,
    r2_send,
    r2_recv,
    r3_send,
    r3_recv,
    h1_recv,
    h2_send,
    h2_recv,
    sib_sems,
    plane_ss,
    plane_rs,
    line_ss,
    line_rs,
):
    operands = (
        (ids_any, ids_ref),
        (cell_any, cell_ref),
        (frac_any, frac_ref),
        (feat_any, feat_ref),
        (weight_any, weight_ref),
        (cot_any, cot_ref),
        (tile_any, tile_ref),
        (bias_any, bias_ref),
    )
    fetches = [
        pltpu.make_async_copy(src, dst, in_sems.at[n])
        for n, (src, dst) in enumerate(operands)
    ]
    planes = side * side
    table_fetches = [
        pltpu.make_async_copy(
            table_any.at[:, pl.ds(q * YZ, YZ)],
            table_ref.at[q],
            in_sems.at[len(operands) + q],
        )
        for q in range(planes)
    ]
    for fetch in fetches[:1] + table_fetches + fetches[1:]:
        fetch.start()
    groups = rows_x * 2
    tiles = cell_ref.shape[0] // 8
    images = ids_ref.shape[0]
    held = table_ref.shape[1] // COEF
    my_x = lax.axis_index("img")
    my_pix = lax.axis_index("pix")
    my_q = my_pix // 2
    my_c = my_pix % 2
    my_g = my_x * 2 + my_c
    my_dev = my_x * (planes * 2) + my_pix

    steps = [(dz, dy) for dz in range(side) for dy in range(side)]
    steps = sorted(steps, key=lambda d: -hops(d[0], side) - hops(d[1], side))[:-1]
    my_z, my_y = my_q // side, my_q % side
    plane_q = [(my_z + dz) % side * side + (my_y + dy) % side for dz, dy in steps]
    steps = [(dx, dc) for dx in range(rows_x) for dc in range(2)]
    steps = sorted(steps, key=lambda d: -2 * hops(d[0], rows_x) - d[1])[:-1]
    line_g = [(my_x + dx) % rows_x * 2 + (my_c + dc) % 2 for dx, dc in steps]

    def plane_dev(q):
        return {"img": my_x, "pix": q * 2 + my_c}

    def line_dev(g):
        return {"img": g // 2, "pix": my_q * 2 + g % 2}

    def plane_copy(stage, q, src, dst, slot=None):
        return pltpu.make_async_remote_copy(
            src_ref=src,
            dst_ref=dst,
            send_sem=plane_ss.at[stage, q],
            recv_sem=plane_rs.at[stage, my_q if slot is None else slot],
            device_id=plane_dev(q),
            device_id_type=MESH,
        )

    def line_copy(stage, g, src, dst, slot=None):
        return pltpu.make_async_remote_copy(
            src_ref=src,
            dst_ref=dst,
            send_sem=line_ss.at[stage, g],
            recv_sem=line_rs.at[stage, my_g if slot is None else slot],
            device_id=line_dev(g),
            device_id_type=MESH,
        )

    def plane_send(stage, src, dst):
        for q in plane_q:
            plane_copy(stage, q, src(q), dst.at[my_q]).start()

    def line_send(stage, src, dst):
        for g in line_g:
            line_copy(stage, g, src(g), dst.at[my_g]).start()

    def plane_arrive(stage, buf):
        for q in plane_q:
            plane_copy(stage, q, buf.at[q], buf.at[q], q).wait_recv()

    def line_arrive(stage, buf):
        for g in line_g:
            line_copy(stage, g, buf.at[g], buf.at[g], g).wait_recv()

    barrier = pltpu.get_barrier_semaphore()
    for q in plane_q:
        pl.semaphore_signal(
            barrier, inc=1, device_id=plane_dev(q), device_id_type=MESH
        )
    for g in line_g:
        pl.semaphore_signal(barrier, inc=1, device_id=line_dev(g), device_id_type=MESH)

    fetches[0].wait()
    holders = []
    ranks = []
    for i in range(images):
        holder = ids_ref[i] // held
        rank = jnp.int32(0)
        for other in holders:
            rank = rank + jnp.where(other == holder, 1, 0)
        holders.append(holder)
        ranks.append(rank)
        hp = holder % (planes * 2)
        holder_q[i] = hp // 2
        holder_g[i] = holder // (planes * 2) * 2 + hp % 2
        rank_ref[i] = rank

    own_row = [jnp.int32(0)] * OWN_MOST
    own_has = [jnp.int32(0)] * OWN_MOST
    for i in range(images):
        for s in range(OWN_MOST):
            hit = (holders[i] == my_dev) & (ranks[i] == s)
            own_row[s] = jnp.where(hit, ids_ref[i] % held, own_row[s])
            own_has[s] = jnp.where(hit, 1, own_has[s])

    for fetch in table_fetches:
        fetch.wait()
    for s in range(OWN_MOST):
        for q in range(planes):
            for k in range(3):
                g1_send[q, s * 9 + 3 * k : s * 9 + 3 * k + 3, :] = table_ref[
                    q, pl.ds(4 * k * held + own_row[s], 3, stride=held), :
                ]
    pl.semaphore_wait(barrier, len(plane_q) + len(line_g))
    plane_send(0, lambda q: g1_send.at[q], g1_recv)
    g1_recv[my_q] = g1_send[my_q]

    def find_dest(q, carry):
        dev = my_x * (planes * 2) + q * 2 + my_c
        for s in range(OWN_MOST):
            found = jnp.int32(images)
            for i in range(images):
                found = jnp.where((holders[i] == dev) & (ranks[i] == s), i, found)
            dest_ref[q * OWN_MOST + s] = found
        return carry

    lax.fori_loop(0, planes, find_dest, 0)

    lane = lax.broadcasted_iota(jnp.int32, (COEF, YZ), 1)
    for s in range(OWN_MOST):
        own = [
            table_ref[q, pl.ds(own_row[s], COEF, stride=held), :]
            for q in range(planes)
        ]
        for q in range(planes):
            here = own[q]
            total = jnp.zeros((COEF, YZ), jnp.float32)
            if q > 0:
                total = total + (here - own[q - 1])
            if q < planes - 1:
                total = total - (own[q + 1] - here)
            for step, first, last in (
                (GZ, lane >= GZ, lane < YZ - GZ),
                (1, lane % GZ != 0, lane % GZ != GZ - 1),
            ):
                before = jnp.where(first, here - pltpu.roll(here, step, 1), 0.0)
                after = jnp.where(last, pltpu.roll(here, YZ - step, 1) - here, 0.0)
                total = total + (before - after)
            tv_ref[q, s * COEF : (s + 1) * COEF, :] = jnp.where(
                own_has[s] == 1, total, 0.0
            )

    acc_ref[...] = jnp.zeros_like(acc_ref)
    head_acc[...] = jnp.zeros_like(head_acc)
    bias_acc[...] = jnp.zeros_like(bias_acc)
    for fetch in fetches[1:]:
        fetch.wait()
    weight_f32 = jnp.concatenate(
        [
            weight_ref[...].astype(jnp.float32),
            jnp.zeros((8 - weight_ref.shape[0], weight_ref.shape[1]), jnp.float32),
        ],
        axis=0,
    )
    weight_rows = weight_f32.astype(jnp.bfloat16)
    weight_cols = (
        jnp.concatenate([weight_f32, jnp.zeros_like(weight_f32)], axis=0)
        .T.astype(jnp.bfloat16)
    )
    chan = lax.broadcasted_iota(jnp.int32, (8, TILE), 0)

    def gather_two():
        plane_arrive(0, g1_recv)
        for i in range(images):
            at = i % IMG_ROW * 9
            g2_send[i // IMG_ROW, at : at + 9, :] = jnp.where(
                rank_ref[i] == 0, g1_recv[holder_q[i], 0:9], g1_recv[holder_q[i], 9:18]
            )
        line_send(0, lambda g: g2_send.at[g // 2], g2_recv)
        g2_recv[my_g] = g2_send[my_x]

    def gather_three():
        line_arrive(0, g2_recv)
        for i in range(IMG_ROW):
            at = i * 9
            g3_send[at : at + 9, :] = g2_recv[
                holder_g[my_x * IMG_ROW + i], at : at + 9
            ]
        plane_send(1, lambda q: g3_send, g3_recv)
        g3_recv[my_q] = g3_send[...]

    def splat_tile(t, carry):
        px = pl.ds(pl.multiple_of(t * TILE, TILE), TILE)
        cell = spread(cell_ref[pl.ds(pl.multiple_of(t * 8, 8), 8), :])
        cx = cell >> 7
        cy = (cell >> 3) & (GY - 1)
        cz = cell & (GZ - 1)
        fx = jnp.broadcast_to(frac_ref[0:1, px], (8, TILE))
        fy = jnp.broadcast_to(frac_ref[1:2, px], (8, TILE))
        fz = jnp.broadcast_to(frac_ref[2:3, px], (8, TILE))
        az = hat(cz, chan, 1.0 - fz, fz)
        gy = 1.0 - fy
        for y in range(0, GY, 2):
            pair = jnp.concatenate(
                [hat(cy, y, gy, fy) * az, hat(cy, y + 1, gy, fy) * az], axis=0
            )
            big = pair.astype(jnp.bfloat16)
            rest = (pair - big.astype(jnp.float32)).astype(jnp.bfloat16)
            splat_ref[t, y * GZ : (y + 2) * GZ, :] = big
            splat_ref[t, YZ + y * GZ : YZ + (y + 2) * GZ, :] = rest
        gx = 1.0 - fx
        ax = jnp.concatenate([hat(cx, chan, gx, fx), hat(cx, chan + 8, gx, fx)], axis=0)
        logits = jnp.dot(
            weight_rows, feat_ref[:, px], preferred_element_type=jnp.float32
        )
        bias = jnp.where(
            chan == 0, bias_ref[0], jnp.where(chan == 1, bias_ref[1], bias_ref[2])
        )
        colour = 1.0 / (1.0 + jnp.exp(-(logits + bias)))
        colour_ref[t] = colour
        parts = []
        for k in range(3):
            u = jnp.broadcast_to(cot_ref[k : k + 1, px].astype(jnp.float32), (GX, TILE))
            uax = u * ax
            uax_ref[t, k * GX : (k + 1) * GX, :] = uax
            for j in range(3):
                col = jnp.broadcast_to(colour[j : j + 1, :], (GX, TILE))
                parts.append((uax * col).astype(jnp.bfloat16))
            parts.append(uax.astype(jnp.bfloat16))
        left = jnp.concatenate(parts, axis=0)
        both = lax.dot_general(
            left, splat_ref[t], NT, preferred_element_type=jnp.float32
        )
        grads = both[:, :YZ] + both[:, YZ:]
        image = tile_ref[t]
        for i in range(IMG_ROW):
            acc_ref[i] += jnp.where(image == i, grads, 0.0)

    def slice_tile(t, carry):
        px = pl.ds(pl.multiple_of(t * TILE, TILE), TILE)
        wide = jnp.dot(
            grid_ref[tile_ref[t]], splat_ref[t], preferred_element_type=jnp.float32
        )
        d_colour = jnp.zeros((8, TILE), jnp.float32)
        for j in range(3):
            total = None
            for k in range(3):
                at = (3 * k + j) * GX
                coef = wide[at : at + GX] + wide[USED + at : USED + at + GX]
                term = coef * uax_ref[t, k * GX : (k + 1) * GX, :]
                total = term if total is None else total + term
            whole = jnp.sum(total, axis=0, keepdims=True)
            d_colour = jnp.where(chan == j, whole, d_colour)
        colour = colour_ref[t]
        d_logits = d_colour * colour * (1.0 - colour)
        d_half = jnp.concatenate([d_logits, jnp.zeros_like(d_logits)], axis=0).astype(
            jnp.bfloat16
        )
        half_ref[t] = d_half
        head_acc[...] += lax.dot_general(
            d_half, feat_ref[:, px], NT, preferred_element_type=jnp.float32
        )
        bias_acc[...] += d_logits

    def run(body, first, last):
        def step(n, carry):
            for m in range(2):
                body(2 * n + m, carry)
            return carry

        lax.fori_loop(first // 2, last // 2, step, 0)

    run(splat_tile, 0, SPLAT_FIRST)
    gather_two()
    run(splat_tile, SPLAT_FIRST, tiles)

    sibling = pltpu.make_async_remote_copy(
        src_ref=acc_ref.at[pl.ds(2 * (1 - my_c), 2)],
        dst_ref=sib_ref,
        send_sem=sib_sems.at[0],
        recv_sem=sib_sems.at[1],
        device_id={"img": my_x, "pix": my_q * 2 + 1 - my_c},
        device_id_type=MESH,
    )
    sibling.start()
    gather_three()
    sibling.wait()
    for i in range(2):
        total_ref[i] = acc_ref[2 * my_c + i] + sib_ref[i]
    for q in range(planes):
        for i in range(2):
            r1_send[q, i * COEF : (i + 1) * COEF, :] = total_ref[
                i, pl.ds(q, COEF, stride=GX), :
            ]
    plane_send(2, lambda q: r1_send.at[q], r1_recv)
    r1_recv[my_q] = r1_send[my_q]

    plane_arrive(1, g3_recv)
    for i in range(IMG_ROW):
        for q in range(planes):
            grid_f32[i, pl.ds(q, 9, stride=GX), :] = g3_recv[q, i * 9 : (i + 1) * 9]
    for i in range(IMG_ROW):
        full = grid_f32[i]
        big = full.astype(jnp.bfloat16)
        rest = (full - big.astype(jnp.float32)).astype(jnp.bfloat16)
        grid_ref[i, 0:USED, 0:YZ] = big
        grid_ref[i, 0:USED, YZ : 2 * YZ] = big
        grid_ref[i, USED : 2 * USED, 0:YZ] = rest
        grid_ref[i, USED : 2 * USED, YZ : 2 * YZ] = rest

    def reduce_two():
        plane_arrive(2, r1_recv)
        total = r1_recv[0]
        for q in range(1, planes):
            total = total + r1_recv[q]
        r2_send[...] = total
        line_send(1, lambda g: r2_send, r2_recv)
        r2_recv[my_g] = total
        r2_recv[groups] = jnp.zeros_like(total)

    def reduce_three():
        line_arrive(1, r2_recv)
        for q in range(planes):
            for s in range(OWN_MOST):
                i = dest_ref[q * OWN_MOST + s]
                r3_send[q, s * COEF : (s + 1) * COEF, :] = jnp.where(
                    i % 2 == 0, r2_recv[i // 2, 0:COEF], r2_recv[i // 2, COEF:]
                )
        plane_send(3, lambda q: r3_send.at[q], r3_recv)
        r3_recv[my_q] = r3_send[my_q]

    run(slice_tile, 0, SLICE_FIRST)
    reduce_two()
    run(slice_tile, SLICE_FIRST, SLICE_SECOND)
    reduce_three()
    run(slice_tile, SLICE_SECOND, tiles)

    bias_sum = jnp.sum(bias_acc[...], axis=1, keepdims=True)
    where_bias = lax.broadcasted_iota(jnp.int32, (8, 128), 0)
    on_lane = lax.broadcasted_iota(jnp.int32, (8, 128), 1)
    bias_row = jnp.sum(
        jnp.where(where_bias == on_lane, bias_sum, 0.0), axis=0, keepdims=True
    )
    head_rows = jnp.concatenate(
        [head_acc[0:8, :], jnp.zeros((8, 128 - head_acc.shape[1]), jnp.float32)], axis=1
    )
    stat_ref[...] = jnp.where(where_bias == 3, bias_row, head_rows)
    plane_send(4, lambda q: stat_ref, h1_recv)
    h1_recv[my_q] = stat_ref[...]

    def feature_tile(t, carry):
        px = pl.ds(pl.multiple_of(t * TILE, TILE), TILE)
        fgrad_ref[:, px] = jnp.dot(
            weight_cols, half_ref[t], preferred_element_type=jnp.float32
        ).astype(jnp.bfloat16)

    run(feature_tile, 0, tiles)
    plane_arrive(4, h1_recv)
    total = h1_recv[0]
    for q in range(1, planes):
        total = total + h1_recv[q]
    h2_send[...] = total
    line_send(2, lambda g: h2_send, h2_recv)
    h2_recv[my_g] = total
    plane_arrive(3, r3_recv)
    for q in range(planes):
        for s in range(OWN_MOST):
            rows = slice(s * COEF, (s + 1) * COEF)
            owned_ref[:, s, q * YZ : (q + 1) * YZ] = r3_recv[q, rows] + tv_ref[q, rows]
    line_arrive(2, h2_recv)
    total = h2_recv[0]
    for g in range(1, groups):
        total = total + h2_recv[g]
    head_ref[...] = total

    for q in plane_q:
        plane_copy(0, q, g1_send.at[q], g1_recv.at[my_q]).wait_send()
        plane_copy(1, q, g3_send, g3_recv.at[my_q]).wait_send()
        plane_copy(2, q, r1_send.at[q], r1_recv.at[my_q]).wait_send()
        plane_copy(3, q, r3_send.at[q], r3_recv.at[my_q]).wait_send()
        plane_copy(4, q, stat_ref, h1_recv.at[my_q]).wait_send()
    for g in line_g:
        line_copy(0, g, g2_send.at[g // 2], g2_recv.at[my_g]).wait_send()
        line_copy(1, g, r2_send, r2_recv.at[my_g]).wait_send()
        line_copy(2, g, h2_send, h2_recv.at[my_g]).wait_send()


def finish(owned_in, stat_in, fgrad_in, owned_ref, head_ref, bias_ref, fgrad_ref, sems):
    copies = [
        pltpu.make_async_copy(fgrad_in, fgrad_ref, sems.at[0]),
        pltpu.make_async_copy(owned_in, owned_ref, sems.at[1]),
    ]
    for copy in copies:
        copy.start()
    head_ref[...] = stat_in[0 : head_ref.shape[0], 0 : head_ref.shape[1]]
    bias_ref[...] = stat_in[3, 0 : bias_ref.shape[0]]
    for copy in copies:
        copy.wait()


def shards(side, rows_x, ids, table, tile_image, cell, frac, feat, weight, bias, cot):
    pixels = cell.shape[0]
    tiles = pixels // TILE
    planes = side * side
    groups = rows_x * 2
    images = ids.shape[0]
    f32, bf16, i32 = jnp.float32, jnp.bfloat16, jnp.int32
    vmem = pl.BlockSpec(memory_space=pltpu.VMEM)
    hbm = pl.BlockSpec(memory_space=pltpu.HBM)
    table_rows = jnp.transpose(table, (1, 0, 2)).reshape(-1, CELLS)
    cell_rows = cell.reshape(pixels // 128, 128)
    owned, stat, fgrad = pl.pallas_call(
        functools.partial(kernel, side, rows_x),
        out_shape=(
            jax.ShapeDtypeStruct((COEF, OWN_MOST, CELLS), f32),
            jax.ShapeDtypeStruct((8, 128), f32),
            jax.ShapeDtypeStruct(feat.shape, bf16),
        ),
        in_specs=[hbm] * 9,
        out_specs=(vmem, vmem, vmem),
        scratch_shapes=[
            pltpu.SMEM(ids.shape, i32),
            pltpu.SMEM(tile_image.shape, i32),
            pltpu.SMEM(bias.shape, f32),
            pltpu.VMEM((planes, table_rows.shape[0], YZ), f32),
            pltpu.VMEM(cell_rows.shape, i32),
            pltpu.VMEM(frac.shape, f32),
            pltpu.VMEM(feat.shape, bf16),
            pltpu.VMEM(weight.shape, bf16),
            pltpu.VMEM(cot.shape, bf16),
            pltpu.SemaphoreType.DMA((8 + planes,)),
            pltpu.VMEM((tiles, 2 * YZ, TILE), bf16),
            pltpu.VMEM((tiles, 3 * GX, TILE), f32),
            pltpu.VMEM((tiles, 8, TILE), f32),
            pltpu.VMEM((tiles, 16, TILE), bf16),
            pltpu.VMEM((IMG_ROW, ROWS, YZ), f32),
            pltpu.VMEM((2, ROWS, YZ), f32),
            pltpu.VMEM((2, ROWS, YZ), f32),
            pltpu.VMEM((IMG_ROW, USED, YZ), f32),
            pltpu.VMEM((IMG_ROW, 2 * USED, 2 * YZ), bf16),
            pltpu.VMEM((planes, OWN_MOST * COEF, YZ), f32),
            pltpu.VMEM((8, 128), f32),
            pltpu.VMEM((16, feat.shape[0]), f32),
            pltpu.VMEM((8, TILE), f32),
            pltpu.SMEM((images,), i32),
            pltpu.SMEM((images,), i32),
            pltpu.SMEM((images,), i32),
            pltpu.SMEM((planes * OWN_MOST,), i32),
            pltpu.VMEM((planes, OWN_MOST * 9, YZ), f32),
            pltpu.VMEM((planes, OWN_MOST * 9, YZ), f32),
            pltpu.VMEM((rows_x, IMG_ROW * 9, YZ), f32),
            pltpu.VMEM((groups, IMG_ROW * 9, YZ), f32),
            pltpu.VMEM((IMG_ROW * 9, YZ), f32),
            pltpu.VMEM((planes, IMG_ROW * 9, YZ), f32),
            pltpu.VMEM((planes, 2 * COEF, YZ), f32),
            pltpu.VMEM((planes, 2 * COEF, YZ), f32),
            pltpu.VMEM((2 * COEF, YZ), f32),
            pltpu.VMEM((groups + 1, 2 * COEF, YZ), f32),
            pltpu.VMEM((planes, OWN_MOST * COEF, YZ), f32),
            pltpu.VMEM((planes, OWN_MOST * COEF, YZ), f32),
            pltpu.VMEM((planes, 8, 128), f32),
            pltpu.VMEM((8, 128), f32),
            pltpu.VMEM((groups, 8, 128), f32),
            pltpu.SemaphoreType.DMA((2,)),
            pltpu.SemaphoreType.DMA((5, planes)),
            pltpu.SemaphoreType.DMA((5, planes)),
            pltpu.SemaphoreType.DMA((3, groups)),
            pltpu.SemaphoreType.DMA((3, groups)),
        ],
        compiler_params=pltpu.CompilerParams(
            collective_id=0, has_side_effects=True, vmem_limit_bytes=VMEM_LIMIT
        ),
    )(
        *(
            pltpu.with_memory_space_constraint(operand, pltpu.HBM)
            for operand in (
                ids,
                tile_image,
                bias,
                table_rows,
                cell_rows,
                frac,
                feat,
                weight,
                cot,
            )
        )
    )
    owned, head, bias_grad, fgrad = pl.pallas_call(
        finish,
        out_shape=(
            jax.ShapeDtypeStruct((COEF, OWN_MOST, CELLS), f32),
            jax.ShapeDtypeStruct(weight.shape, f32),
            jax.ShapeDtypeStruct(bias.shape, f32),
            jax.ShapeDtypeStruct(feat.shape, bf16),
        ),
        in_specs=[vmem, vmem, vmem],
        out_specs=(hbm, vmem, vmem, hbm),
        scratch_shapes=[pltpu.SemaphoreType.DMA((2,))],
        compiler_params=pltpu.CompilerParams(vmem_limit_bytes=16 << 20),
    )(owned, stat, fgrad)
    return jnp.transpose(owned, (1, 0, 2)), head, bias_grad, fgrad


def solution(mesh):
    rows_x = mesh.shape["img"]
    side = math.isqrt(mesh.shape["pix"] // 2)
    return jax.shard_map(
        functools.partial(shards, side, rows_x),
        mesh=mesh,
        in_specs=(
            P(),
            P(("img", "pix"), None, None),
            P(("img", "pix")),
            P(("img", "pix")),
            P(None, ("img", "pix")),
            P(None, ("img", "pix")),
            P(),
            P(),
            P(None, ("img", "pix")),
        ),
        out_specs=(P(("img", "pix"), None, None), P(), P(), P(None, ("img", "pix"))),
        check_vma=False,
    )
```

```python
import functools
import math

import jax
import jax.numpy as jnp
from jax import lax
from jax.experimental import pallas as pl
from jax.experimental.pallas import tpu as pltpu
from jax.sharding import PartitionSpec as P

GX = 16
GY = 16
GZ = 8
YZ = GY * GZ
CELLS = GX * YZ
COEF = 12
TILE = 1024
IMG_ROW = 4
OWN_MOST = 2
ROWS = COEF * GX
USED = 9 * GX
VMEM_LIMIT = 40 << 20
SPLAT_UNROLL = 8
SLICE_UNROLL = 16
FEATURE_UNROLL = 8
MESH = pl.DeviceIdType.MESH
NT = (((1,), (1,)), ((), ()))


def spread(block):
    return jnp.concatenate(
        [jnp.broadcast_to(block[s : s + 1, :], (8, 128)) for s in range(8)], axis=1
    )


def hat(coord, level, low, high):
    return jnp.where(coord == level, low, jnp.where(coord == level - 1, high, 0.0))


def hops(a, b):
    return min(a % b, -a % b)


def kernel(
    side,
    rows_x,
    ids_any,
    tile_any,
    bias_any,
    table_any,
    cell_any,
    frac_any,
    feat_any,
    weight_any,
    cot_any,
    owned_ref,
    head_ref,
    fgrad_ref,
    ids_ref,
    tile_ref,
    bias_ref,
    table_ref,
    cell_ref,
    frac_ref,
    feat_ref,
    weight_ref,
    cot_ref,
    in_sems,
    splat_ref,
    uax_ref,
    colour_ref,
    half_ref,
    acc_ref,
    sib_ref,
    total_ref,
    grid_f32,
    grid_ref,
    tv_ref,
    stat_ref,
    bias_acc,
    holder_q,
    holder_g,
    rank_ref,
    dest_ref,
    g1_send,
    g1_recv,
    g2_send,
    g2_recv,
    g3_send,
    g3_recv,
    r1_send,
    r1_recv,
    r2_send,
    r2_recv,
    r3_send,
    r3_recv,
    h1_recv,
    head_sems,
    sib_sems,
    plane_ss,
    plane_rs,
    line_ss,
    line_rs,
):
    operands = (
        (ids_any, ids_ref),
        (cell_any, cell_ref),
        (frac_any, frac_ref),
        (feat_any, feat_ref),
        (weight_any, weight_ref),
        (cot_any, cot_ref),
        (tile_any, tile_ref),
        (bias_any, bias_ref),
    )
    fetches = [
        pltpu.make_async_copy(src, dst, in_sems.at[n])
        for n, (src, dst) in enumerate(operands)
    ]
    planes = side * side
    table_fetches = [
        pltpu.make_async_copy(
            table_any.at[:, pl.ds(q * YZ, YZ)],
            table_ref.at[q],
            in_sems.at[len(operands) + q],
        )
        for q in range(planes)
    ]
    groups = rows_x * 2
    tiles = cell_ref.shape[0] // 8
    images = ids_ref.shape[0]
    held = table_ref.shape[1] // COEF
    my_x = lax.axis_index("img")
    my_pix = lax.axis_index("pix")
    my_q = my_pix // 2
    my_c = my_pix % 2
    my_g = my_x * 2 + my_c
    my_dev = my_x * (planes * 2) + my_pix

    steps = [(dz, dy) for dz in range(side) for dy in range(side)]
    steps = sorted(steps, key=lambda d: -hops(d[0], side) - hops(d[1], side))[:-1]
    my_z, my_y = my_q // side, my_q % side
    plane_q = [(my_z + dz) % side * side + (my_y + dy) % side for dz, dy in steps]
    steps = [(dx, dc) for dx in range(rows_x) for dc in range(2)]
    steps = sorted(steps, key=lambda d: -2 * hops(d[0], rows_x) - d[1])[:-1]
    line_g = [(my_x + dx) % rows_x * 2 + (my_c + dc) % 2 for dx, dc in steps]

    def plane_dev(q):
        return {"img": my_x, "pix": q * 2 + my_c}

    def line_dev(g):
        return {"img": g // 2, "pix": my_q * 2 + g % 2}

    def plane_copy(stage, q, src, dst, slot=None):
        return pltpu.make_async_remote_copy(
            src_ref=src,
            dst_ref=dst,
            send_sem=plane_ss.at[stage, q],
            recv_sem=plane_rs.at[stage, my_q if slot is None else slot],
            device_id=plane_dev(q),
            device_id_type=MESH,
        )

    def line_copy(stage, g, src, dst, slot=None):
        return pltpu.make_async_remote_copy(
            src_ref=src,
            dst_ref=dst,
            send_sem=line_ss.at[stage, g],
            recv_sem=line_rs.at[stage, my_g if slot is None else slot],
            device_id=line_dev(g),
            device_id_type=MESH,
        )

    steps = [
        (dx, dz, dy, dc)
        for dx in range(rows_x)
        for dz in range(side)
        for dy in range(side)
        for dc in range(2)
    ]
    far = [hops(dx, rows_x) + hops(dz, side) + hops(dy, side) for dx, dz, dy, _ in steps]
    order = sorted(range(len(steps)), key=lambda n: -2 * far[n] - steps[n][3])[:-1]
    head_devs = []
    for dx, dz, dy, dc in [steps[n] for n in order]:
        q = (my_z + dz) % side * side + (my_y + dy) % side
        head_devs.append(
            {"img": (my_x + dx) % rows_x, "pix": q * 2 + (my_c + dc) % 2}
        )

    def head_copy(dev):
        return pltpu.make_async_remote_copy(
            src_ref=stat_ref,
            dst_ref=h1_recv.at[my_dev],
            send_sem=head_sems.at[0],
            recv_sem=head_sems.at[1],
            device_id=dev,
            device_id_type=MESH,
        )

    def plane_send(stage, src, dst):
        for q in plane_q:
            plane_copy(stage, q, src(q), dst.at[my_q]).start()

    def line_send(stage, src, dst):
        for g in line_g:
            line_copy(stage, g, src(g), dst.at[my_g]).start()

    def plane_arrive(stage, buf):
        for q in plane_q:
            plane_copy(stage, q, buf.at[q], buf.at[q], q).wait_recv()

    def line_arrive(stage, buf):
        for g in line_g:
            line_copy(stage, g, buf.at[g], buf.at[g], g).wait_recv()

    barrier = pltpu.get_barrier_semaphore()
    for q in plane_q:
        pl.semaphore_signal(
            barrier, inc=1, device_id=plane_dev(q), device_id_type=MESH
        )
    for g in line_g:
        pl.semaphore_signal(barrier, inc=1, device_id=line_dev(g), device_id_type=MESH)

    for fetch in fetches[:1] + table_fetches + fetches[1:]:
        fetch.start()

    acc_ref[...] = jnp.zeros_like(acc_ref)
    bias_acc[...] = jnp.zeros_like(bias_acc)
    fetches[0].wait()
    holders = []
    ranks = []
    for i in range(images):
        holder = ids_ref[i] // held
        rank = jnp.int32(0)
        for other in holders:
            rank = rank + jnp.where(other == holder, 1, 0)
        holders.append(holder)
        ranks.append(rank)
        hp = holder % (planes * 2)
        holder_q[i] = hp // 2
        holder_g[i] = holder // (planes * 2) * 2 + hp % 2
        rank_ref[i] = rank

    own_row = [jnp.int32(0)] * OWN_MOST
    own_has = [jnp.int32(0)] * OWN_MOST
    for i in range(images):
        for s in range(OWN_MOST):
            hit = (holders[i] == my_dev) & (ranks[i] == s)
            own_row[s] = jnp.where(hit, ids_ref[i] % held, own_row[s])
            own_has[s] = jnp.where(hit, 1, own_has[s])

    for fetch in table_fetches:
        fetch.wait()
    for s in range(OWN_MOST):
        for q in range(planes):
            for k in range(3):
                g1_send[q, s * 9 + 3 * k : s * 9 + 3 * k + 3, :] = table_ref[
                    q, pl.ds(4 * k * held + own_row[s], 3, stride=held), :
                ]
    pl.semaphore_wait(barrier, len(plane_q) + len(line_g))
    plane_send(0, lambda q: g1_send.at[q], g1_recv)
    g1_recv[my_q] = g1_send[my_q]

    for fetch in fetches[1:]:
        fetch.wait()
    weight_f32 = jnp.concatenate(
        [
            weight_ref[...].astype(jnp.float32),
            jnp.zeros((8 - weight_ref.shape[0], weight_ref.shape[1]), jnp.float32),
        ],
        axis=0,
    )
    weight_rows = weight_f32.astype(jnp.bfloat16)
    weight_cols = (
        jnp.concatenate([weight_f32, jnp.zeros_like(weight_f32)], axis=0)
        .T.astype(jnp.bfloat16)
    )
    chan = lax.broadcasted_iota(jnp.int32, (8, TILE), 0)

    def gather_two():
        plane_arrive(0, g1_recv)
        for i in range(images):
            at = i % IMG_ROW * 9
            g2_send[i // IMG_ROW, at : at + 9, :] = jnp.where(
                rank_ref[i] == 0, g1_recv[holder_q[i], 0:9], g1_recv[holder_q[i], 9:18]
            )
        line_send(0, lambda g: g2_send.at[g // 2], g2_recv)
        g2_recv[my_g] = g2_send[my_x]

    def gather_three():
        line_arrive(0, g2_recv)
        for i in range(IMG_ROW):
            at = i * 9
            g3_send[at : at + 9, :] = g2_recv[
                holder_g[my_x * IMG_ROW + i], at : at + 9
            ]
        plane_send(1, lambda q: g3_send, g3_recv)
        g3_recv[my_q] = g3_send[...]

    def splat_tile(t):
        px = pl.ds(pl.multiple_of(t * TILE, TILE), TILE)
        cell = spread(cell_ref[pl.ds(pl.multiple_of(t * 8, 8), 8), :])
        cx = cell >> 7
        cy = (cell >> 3) & (GY - 1)
        cz = cell & (GZ - 1)
        fx = jnp.broadcast_to(frac_ref[0:1, px], (8, TILE))
        fy = jnp.broadcast_to(frac_ref[1:2, px], (8, TILE))
        fz = jnp.broadcast_to(frac_ref[2:3, px], (8, TILE))
        az = hat(cz, chan, 1.0 - fz, fz)
        gy = 1.0 - fy
        for y in range(0, GY, 2):
            pair = jnp.concatenate(
                [hat(cy, y, gy, fy) * az, hat(cy, y + 1, gy, fy) * az], axis=0
            )
            big = pair.astype(jnp.bfloat16)
            rest = (pair - big.astype(jnp.float32)).astype(jnp.bfloat16)
            splat_ref[t, y * GZ : (y + 2) * GZ, :] = big
            splat_ref[t, YZ + y * GZ : YZ + (y + 2) * GZ, :] = rest
        gx = 1.0 - fx
        ax = jnp.concatenate([hat(cx, chan, gx, fx), hat(cx, chan + 8, gx, fx)], axis=0)
        logits = jnp.dot(
            weight_rows, feat_ref[:, px], preferred_element_type=jnp.float32
        )
        bias = jnp.where(
            chan == 0, bias_ref[0], jnp.where(chan == 1, bias_ref[1], bias_ref[2])
        )
        colour = 1.0 / (1.0 + jnp.exp(-(logits + bias)))
        colour_ref[t] = colour
        parts = []
        for k in range(3):
            u = jnp.broadcast_to(cot_ref[k : k + 1, px].astype(jnp.float32), (GX, TILE))
            uax = u * ax
            uax_ref[t, k * GX : (k + 1) * GX, :] = uax
            for j in range(3):
                col = jnp.broadcast_to(colour[j : j + 1, :], (GX, TILE))
                parts.append((uax * col).astype(jnp.bfloat16))
            parts.append(uax.astype(jnp.bfloat16))
        left = jnp.concatenate(parts, axis=0)
        both = lax.dot_general(
            left, splat_ref[t], NT, preferred_element_type=jnp.float32
        )
        grads = both[:, :YZ] + both[:, YZ:]
        image = tile_ref[t]
        for i in range(IMG_ROW):
            acc_ref[i] += jnp.where(image == i, grads, 0.0)

    def slice_tile(t):
        px = pl.ds(pl.multiple_of(t * TILE, TILE), TILE)
        wide = jnp.dot(
            grid_ref[tile_ref[t]], splat_ref[t], preferred_element_type=jnp.float32
        )
        d_colour = jnp.zeros((8, TILE), jnp.float32)
        for j in range(3):
            total = None
            for k in range(3):
                at = (3 * k + j) * GX
                coef = wide[at : at + GX] + wide[USED + at : USED + at + GX]
                term = coef * uax_ref[t, k * GX : (k + 1) * GX, :]
                total = term if total is None else total + term
            whole = jnp.sum(total, axis=0, keepdims=True)
            d_colour = jnp.where(chan == j, whole, d_colour)
        colour = colour_ref[t]
        d_logits = d_colour * colour * (1.0 - colour)
        d_half = jnp.concatenate([d_logits, jnp.zeros_like(d_logits)], axis=0).astype(
            jnp.bfloat16
        )
        half_ref[:, px] = d_half
        bias_acc[...] += d_logits

    def run(body, unroll):
        def step(n, carry):
            for m in range(unroll):
                body(unroll * n + m)
            return carry

        lax.fori_loop(0, tiles // unroll, step, 0)

    run(splat_tile, SPLAT_UNROLL)

    sibling = pltpu.make_async_remote_copy(
        src_ref=acc_ref.at[pl.ds(2 * (1 - my_c), 2)],
        dst_ref=sib_ref,
        send_sem=sib_sems.at[0],
        recv_sem=sib_sems.at[1],
        device_id={"img": my_x, "pix": my_q * 2 + 1 - my_c},
        device_id_type=MESH,
    )
    sibling.start()
    gather_two()
    sibling.wait()
    for i in range(2):
        total_ref[i] = acc_ref[2 * my_c + i] + sib_ref[i]
    for q in range(planes):
        for i in range(2):
            r1_send[q, i * COEF : (i + 1) * COEF, :] = total_ref[
                i, pl.ds(q, COEF, stride=GX), :
            ]
    plane_send(2, lambda q: r1_send.at[q], r1_recv)
    r1_recv[my_q] = r1_send[my_q]

    gather_three()

    def find_dest(q, carry):
        dev = my_x * (planes * 2) + q * 2 + my_c
        for s in range(OWN_MOST):
            found = jnp.int32(images)
            for i in range(images):
                found = jnp.where((holders[i] == dev) & (ranks[i] == s), i, found)
            dest_ref[q * OWN_MOST + s] = found
        return carry

    lax.fori_loop(0, planes, find_dest, 0)

    lane = lax.broadcasted_iota(jnp.int32, (COEF, YZ), 1)
    for s in range(OWN_MOST):
        own = [
            table_ref[q, pl.ds(own_row[s], COEF, stride=held), :]
            for q in range(planes)
        ]
        for q in range(planes):
            here = own[q]
            total = jnp.zeros((COEF, YZ), jnp.float32)
            if q > 0:
                total = total + (here - own[q - 1])
            if q < planes - 1:
                total = total - (own[q + 1] - here)
            for step, first, last in (
                (GZ, lane >= GZ, lane < YZ - GZ),
                (1, lane % GZ != 0, lane % GZ != GZ - 1),
            ):
                before = jnp.where(first, here - pltpu.roll(here, step, 1), 0.0)
                after = jnp.where(last, pltpu.roll(here, YZ - step, 1) - here, 0.0)
                total = total + (before - after)
            tv_ref[q, s * COEF : (s + 1) * COEF, :] = jnp.where(
                own_has[s] == 1, total, 0.0
            )

    def reduce_two():
        plane_arrive(2, r1_recv)
        total = r1_recv[0]
        for q in range(1, planes):
            total = total + r1_recv[q]
        r2_send[...] = total
        line_send(1, lambda g: r2_send, r2_recv)
        r2_recv[my_g] = total
        r2_recv[groups] = jnp.zeros_like(total)

    def reduce_three():
        line_arrive(1, r2_recv)
        for q in range(planes):
            for s in range(OWN_MOST):
                i = dest_ref[q * OWN_MOST + s]
                r3_send[q, s * COEF : (s + 1) * COEF, :] = jnp.where(
                    i % 2 == 0, r2_recv[i // 2, 0:COEF], r2_recv[i // 2, COEF:]
                )
        plane_send(3, lambda q: r3_send.at[q], r3_recv)
        r3_recv[my_q] = r3_send[my_q]

    reduce_two()
    plane_arrive(1, g3_recv)
    for i in range(IMG_ROW):
        for q in range(planes):
            grid_f32[i, pl.ds(q, 9, stride=GX), :] = g3_recv[q, i * 9 : (i + 1) * 9]
    for i in range(IMG_ROW):
        full = grid_f32[i]
        big = full.astype(jnp.bfloat16)
        rest = (full - big.astype(jnp.float32)).astype(jnp.bfloat16)
        grid_ref[i, 0:USED, 0:YZ] = big
        grid_ref[i, 0:USED, YZ : 2 * YZ] = big
        grid_ref[i, USED : 2 * USED, 0:YZ] = rest
        grid_ref[i, USED : 2 * USED, YZ : 2 * YZ] = rest

    run(slice_tile, SLICE_UNROLL)

    head = lax.dot_general(
        half_ref[...], feat_ref[...], NT, preferred_element_type=jnp.float32
    )
    bias_sum = jnp.sum(bias_acc[...], axis=1, keepdims=True)
    on_row = lax.broadcasted_iota(jnp.int32, (8, head.shape[1]), 0)
    on_lane = lax.broadcasted_iota(jnp.int32, (8, head.shape[1]), 1)
    bias_row = jnp.sum(
        jnp.where(on_row == on_lane, bias_sum, 0.0), axis=0, keepdims=True
    )
    stat_ref[0:1, :] = jnp.concatenate([head[0:1], head[1:2]], axis=1)
    stat_ref[1:2, :] = jnp.concatenate([head[2:3], bias_row], axis=1)
    own_stat = pltpu.make_async_copy(stat_ref, h1_recv.at[my_dev], head_sems.at[1])
    own_stat.start()
    for dev in head_devs:
        head_copy(dev).start()
    reduce_three()

    def feature_tile(t):
        px = pl.ds(pl.multiple_of(t * TILE, TILE), TILE)
        fgrad_ref[:, px] = jnp.dot(
            weight_cols, half_ref[:, px], preferred_element_type=jnp.float32
        ).astype(jnp.bfloat16)

    run(feature_tile, FEATURE_UNROLL)
    plane_arrive(3, r3_recv)
    for q in range(planes):
        for s in range(OWN_MOST):
            rows = slice(s * COEF, (s + 1) * COEF)
            owned_ref[:, s, q * YZ : (q + 1) * YZ] = r3_recv[q, rows] + tv_ref[q, rows]
    pltpu.make_async_copy(h1_recv, h1_recv, head_sems.at[1]).wait()
    head_ref[...] = jnp.sum(h1_recv[...], axis=0)

    for q in plane_q:
        plane_copy(0, q, g1_send.at[q], g1_recv.at[my_q]).wait_send()
        plane_copy(1, q, g3_send, g3_recv.at[my_q]).wait_send()
        plane_copy(2, q, r1_send.at[q], r1_recv.at[my_q]).wait_send()
        plane_copy(3, q, r3_send.at[q], r3_recv.at[my_q]).wait_send()
    for g in line_g:
        line_copy(0, g, g2_send.at[g // 2], g2_recv.at[my_g]).wait_send()
        line_copy(1, g, r2_send, r2_recv.at[my_g]).wait_send()
    sent = h1_recv.at[pl.ds(0, len(head_devs))]
    pltpu.make_async_copy(sent, sent, head_sems.at[0]).wait()


def finish(
    owned_in,
    stat_in,
    fgrad_in,
    owned_out,
    head_out,
    bias_out,
    fgrad_out,
    head_ref,
    bias_ref,
    sems,
):
    parts = 4
    rows = fgrad_in.shape[0] // parts
    copies = [
        (fgrad_in.at[pl.ds(n * rows, rows)], fgrad_out.at[pl.ds(n * rows, rows)])
        for n in range(parts)
    ]
    copies += [(owned_in, owned_out), (head_ref, head_out), (bias_ref, bias_out)]
    copies = [
        pltpu.make_async_copy(src, dst, sems.at[n])
        for n, (src, dst) in enumerate(copies)
    ]
    for copy in copies[:-2]:
        copy.start()
    width = head_ref.shape[1]
    head_ref[0:1, :] = stat_in[0:1, 0:width]
    head_ref[1:2, :] = stat_in[0:1, width : 2 * width]
    head_ref[2:3, :] = stat_in[1:2, 0:width]
    bias_ref[...] = stat_in[1, width : width + bias_ref.shape[0]]
    for copy in copies[-2:]:
        copy.start()
    for copy in copies:
        copy.wait()


def shards(side, rows_x, ids, table, tile_image, cell, frac, feat, weight, bias, cot):
    pixels = cell.shape[0]
    tiles = pixels // TILE
    planes = side * side
    groups = rows_x * 2
    images = ids.shape[0]
    f32, bf16, i32 = jnp.float32, jnp.bfloat16, jnp.int32
    vmem = pl.BlockSpec(memory_space=pltpu.VMEM)
    hbm = pl.BlockSpec(memory_space=pltpu.HBM)
    table_rows = jnp.transpose(table, (1, 0, 2)).reshape(-1, CELLS)
    cell_rows = cell.reshape(pixels // 128, 128)
    owned, stat, fgrad = pl.pallas_call(
        functools.partial(kernel, side, rows_x),
        out_shape=(
            jax.ShapeDtypeStruct((COEF, OWN_MOST, CELLS), f32),
            jax.ShapeDtypeStruct((2, 128), f32),
            jax.ShapeDtypeStruct(feat.shape, bf16),
        ),
        in_specs=[hbm] * 9,
        out_specs=(vmem, vmem, vmem),
        scratch_shapes=[
            pltpu.SMEM(ids.shape, i32),
            pltpu.SMEM(tile_image.shape, i32),
            pltpu.SMEM(bias.shape, f32),
            pltpu.VMEM((planes, table_rows.shape[0], YZ), f32),
            pltpu.VMEM(cell_rows.shape, i32),
            pltpu.VMEM(frac.shape, f32),
            pltpu.VMEM(feat.shape, bf16),
            pltpu.VMEM(weight.shape, bf16),
            pltpu.VMEM(cot.shape, bf16),
            pltpu.SemaphoreType.DMA((8 + planes,)),
            pltpu.VMEM((tiles, 2 * YZ, TILE), bf16),
            pltpu.VMEM((tiles, 3 * GX, TILE), f32),
            pltpu.VMEM((tiles, 8, TILE), f32),
            pltpu.VMEM((16, pixels), bf16),
            pltpu.VMEM((IMG_ROW, ROWS, YZ), f32),
            pltpu.VMEM((2, ROWS, YZ), f32),
            pltpu.VMEM((2, ROWS, YZ), f32),
            pltpu.VMEM((IMG_ROW, USED, YZ), f32),
            pltpu.VMEM((IMG_ROW, 2 * USED, 2 * YZ), bf16),
            pltpu.VMEM((planes, OWN_MOST * COEF, YZ), f32),
            pltpu.VMEM((2, 128), f32),
            pltpu.VMEM((8, TILE), f32),
            pltpu.SMEM((images,), i32),
            pltpu.SMEM((images,), i32),
            pltpu.SMEM((images,), i32),
            pltpu.SMEM((planes * OWN_MOST,), i32),
            pltpu.VMEM((planes, OWN_MOST * 9, YZ), f32),
            pltpu.VMEM((planes, OWN_MOST * 9, YZ), f32),
            pltpu.VMEM((rows_x, IMG_ROW * 9, YZ), f32),
            pltpu.VMEM((groups, IMG_ROW * 9, YZ), f32),
            pltpu.VMEM((IMG_ROW * 9, YZ), f32),
            pltpu.VMEM((planes, IMG_ROW * 9, YZ), f32),
            pltpu.VMEM((planes, 2 * COEF, YZ), f32),
            pltpu.VMEM((planes, 2 * COEF, YZ), f32),
            pltpu.VMEM((2 * COEF, YZ), f32),
            pltpu.VMEM((groups + 1, 2 * COEF, YZ), f32),
            pltpu.VMEM((planes, OWN_MOST * COEF, YZ), f32),
            pltpu.VMEM((planes, OWN_MOST * COEF, YZ), f32),
            pltpu.VMEM((planes * groups, 2, 128), f32),
            pltpu.SemaphoreType.DMA((2,)),
            pltpu.SemaphoreType.DMA((2,)),
            pltpu.SemaphoreType.DMA((4, planes)),
            pltpu.SemaphoreType.DMA((4, planes)),
            pltpu.SemaphoreType.DMA((2, groups)),
            pltpu.SemaphoreType.DMA((2, groups)),
        ],
        compiler_params=pltpu.CompilerParams(
            collective_id=0, has_side_effects=True, vmem_limit_bytes=VMEM_LIMIT
        ),
    )(
        *(
            pltpu.with_memory_space_constraint(operand, pltpu.HBM)
            for operand in (
                ids,
                tile_image,
                bias,
                table_rows,
                cell_rows,
                frac,
                feat,
                weight,
                cot,
            )
        )
    )
    owned, head, bias_grad, fgrad = pl.pallas_call(
        finish,
        out_shape=(
            jax.ShapeDtypeStruct((COEF, OWN_MOST, CELLS), f32),
            jax.ShapeDtypeStruct(weight.shape, f32),
            jax.ShapeDtypeStruct(bias.shape, f32),
            jax.ShapeDtypeStruct(feat.shape, bf16),
        ),
        in_specs=[vmem, vmem, vmem],
        out_specs=(hbm, hbm, hbm, hbm),
        scratch_shapes=[
            pltpu.VMEM(weight.shape, f32),
            pltpu.VMEM(bias.shape, f32),
            pltpu.SemaphoreType.DMA((7,)),
        ],
        compiler_params=pltpu.CompilerParams(vmem_limit_bytes=16 << 20),
    )(owned, stat, fgrad)
    return jnp.transpose(owned, (1, 0, 2)), head, bias_grad, fgrad


def solution(mesh):
    rows_x = mesh.shape["img"]
    side = math.isqrt(mesh.shape["pix"] // 2)
    return jax.shard_map(
        functools.partial(shards, side, rows_x),
        mesh=mesh,
        in_specs=(
            P(),
            P(("img", "pix"), None, None),
            P(("img", "pix")),
            P(("img", "pix")),
            P(None, ("img", "pix")),
            P(None, ("img", "pix")),
            P(),
            P(),
            P(None, ("img", "pix")),
        ),
        out_specs=(P(("img", "pix"), None, None), P(), P(), P(None, ("img", "pix"))),
        check_vma=False,
    )
```

```python
import functools
import math

import jax
import jax.numpy as jnp
from jax import lax
from jax.experimental import pallas as pl
from jax.experimental.pallas import tpu as pltpu
from jax.sharding import PartitionSpec as P

GX = 16
GY = 16
GZ = 8
YZ = GY * GZ
CELLS = GX * YZ
COEF = 12
TILE = 1024
IMG_ROW = 4
OWN_MOST = 2
ROWS = COEF * GX
USED = 9 * GX
VMEM_LIMIT = 40 << 20
SPLAT_UNROLL = 8
FEATURE_UNROLL = 8
MESH = pl.DeviceIdType.MESH
NT = (((1,), (1,)), ((), ()))


def spread(block):
    return jnp.concatenate(
        [jnp.broadcast_to(block[s : s + 1, :], (8, 128)) for s in range(8)], axis=1
    )


def hat(coord, level, low, high):
    return jnp.where(coord == level, low, jnp.where(coord == level - 1, high, 0.0))


def hops(a, b):
    return min(a % b, -a % b)


def kernel(
    side,
    rows_x,
    ids_any,
    tile_any,
    bias_any,
    table_any,
    cell_any,
    frac_any,
    feat_any,
    weight_any,
    cot_any,
    owned_ref,
    head_ref,
    fgrad_ref,
    ids_ref,
    tile_ref,
    bias_ref,
    table_ref,
    cell_ref,
    frac_ref,
    feat_ref,
    weight_ref,
    cot_ref,
    in_sems,
    splat_ref,
    uax_ref,
    colour_ref,
    half_ref,
    feat_t_ref,
    acc_ref,
    sib_ref,
    total_ref,
    grid_f32,
    grid_ref,
    tv_ref,
    stat_ref,
    holder_q,
    holder_g,
    rank_ref,
    dest_ref,
    g1_send,
    g1_recv,
    g2_send,
    g2_recv,
    g3_send,
    g3_recv,
    r1_send,
    r1_recv,
    r2_send,
    r2_recv,
    r3_send,
    r3_recv,
    h1_recv,
    head_sems,
    sib_sems,
    plane_ss,
    plane_rs,
    line_ss,
    line_rs,
):
    operands = (
        (ids_any, ids_ref),
        (cell_any, cell_ref),
        (frac_any, frac_ref),
        (feat_any, feat_ref),
        (weight_any, weight_ref),
        (cot_any, cot_ref),
        (tile_any, tile_ref),
        (bias_any, bias_ref),
    )
    fetches = [
        pltpu.make_async_copy(src, dst, in_sems.at[n])
        for n, (src, dst) in enumerate(operands)
    ]
    planes = side * side
    table_fetches = [
        pltpu.make_async_copy(
            table_any.at[:, pl.ds(q * YZ, YZ)],
            table_ref.at[q],
            in_sems.at[len(operands) + q],
        )
        for q in range(planes)
    ]
    groups = rows_x * 2
    tiles = cell_ref.shape[0] // 8
    images = ids_ref.shape[0]
    held = table_ref.shape[1] // COEF
    my_x = lax.axis_index("img")
    my_pix = lax.axis_index("pix")
    my_q = my_pix // 2
    my_c = my_pix % 2
    my_g = my_x * 2 + my_c
    my_dev = my_x * (planes * 2) + my_pix

    steps = [(dz, dy) for dz in range(side) for dy in range(side)]
    steps = sorted(steps, key=lambda d: -hops(d[0], side) - hops(d[1], side))[:-1]
    my_z, my_y = my_q // side, my_q % side
    plane_q = [(my_z + dz) % side * side + (my_y + dy) % side for dz, dy in steps]
    steps = [(dx, dc) for dx in range(rows_x) for dc in range(2)]
    steps = sorted(steps, key=lambda d: -2 * hops(d[0], rows_x) - d[1])[:-1]
    line_g = [(my_x + dx) % rows_x * 2 + (my_c + dc) % 2 for dx, dc in steps]

    def plane_dev(q):
        return {"img": my_x, "pix": q * 2 + my_c}

    def line_dev(g):
        return {"img": g // 2, "pix": my_q * 2 + g % 2}

    def plane_copy(stage, q, src, dst, slot=None):
        return pltpu.make_async_remote_copy(
            src_ref=src,
            dst_ref=dst,
            send_sem=plane_ss.at[stage, q],
            recv_sem=plane_rs.at[stage, my_q if slot is None else slot],
            device_id=plane_dev(q),
            device_id_type=MESH,
        )

    def line_copy(stage, g, src, dst, slot=None):
        return pltpu.make_async_remote_copy(
            src_ref=src,
            dst_ref=dst,
            send_sem=line_ss.at[stage, g],
            recv_sem=line_rs.at[stage, my_g if slot is None else slot],
            device_id=line_dev(g),
            device_id_type=MESH,
        )

    steps = [
        (dx, dz, dy, dc)
        for dx in range(rows_x)
        for dz in range(side)
        for dy in range(side)
        for dc in range(2)
    ]
    far = [hops(dx, rows_x) + hops(dz, side) + hops(dy, side) for dx, dz, dy, _ in steps]
    order = sorted(range(len(steps)), key=lambda n: -2 * far[n] - steps[n][3])[:-1]
    head_devs = []
    for dx, dz, dy, dc in [steps[n] for n in order]:
        q = (my_z + dz) % side * side + (my_y + dy) % side
        head_devs.append(
            {"img": (my_x + dx) % rows_x, "pix": q * 2 + (my_c + dc) % 2}
        )

    def head_copy(dev):
        return pltpu.make_async_remote_copy(
            src_ref=stat_ref,
            dst_ref=h1_recv.at[my_dev],
            send_sem=head_sems.at[0],
            recv_sem=head_sems.at[1],
            device_id=dev,
            device_id_type=MESH,
        )

    def plane_send(stage, src, dst):
        for q in plane_q:
            plane_copy(stage, q, src(q), dst.at[my_q]).start()

    def line_send(stage, src, dst):
        for g in line_g:
            line_copy(stage, g, src(g), dst.at[my_g]).start()

    def plane_arrive(stage, buf):
        for q in plane_q:
            plane_copy(stage, q, buf.at[q], buf.at[q], q).wait_recv()

    def line_arrive(stage, buf):
        for g in line_g:
            line_copy(stage, g, buf.at[g], buf.at[g], g).wait_recv()

    barrier = pltpu.get_barrier_semaphore()
    for q in plane_q:
        pl.semaphore_signal(
            barrier, inc=1, device_id=plane_dev(q), device_id_type=MESH
        )
    for g in line_g:
        pl.semaphore_signal(barrier, inc=1, device_id=line_dev(g), device_id_type=MESH)

    for fetch in fetches[:1] + table_fetches + fetches[1:]:
        fetch.start()

    acc_ref[...] = jnp.zeros_like(acc_ref)
    fetches[0].wait()
    holders = []
    ranks = []
    for i in range(images):
        holder = ids_ref[i] // held
        rank = jnp.int32(0)
        for other in holders:
            rank = rank + jnp.where(other == holder, 1, 0)
        holders.append(holder)
        ranks.append(rank)
        hp = holder % (planes * 2)
        holder_q[i] = hp // 2
        holder_g[i] = holder // (planes * 2) * 2 + hp % 2
        rank_ref[i] = rank

    own_row = [jnp.int32(0)] * OWN_MOST
    own_has = [jnp.int32(0)] * OWN_MOST
    for i in range(images):
        for s in range(OWN_MOST):
            hit = (holders[i] == my_dev) & (ranks[i] == s)
            own_row[s] = jnp.where(hit, ids_ref[i] % held, own_row[s])
            own_has[s] = jnp.where(hit, 1, own_has[s])

    for fetch in table_fetches:
        fetch.wait()
    for s in range(OWN_MOST):
        for q in range(planes):
            for k in range(3):
                g1_send[q, s * 9 + 3 * k : s * 9 + 3 * k + 3, :] = table_ref[
                    q, pl.ds(4 * k * held + own_row[s], 3, stride=held), :
                ]
    pl.semaphore_wait(barrier, len(plane_q) + len(line_g))
    plane_send(0, lambda q: g1_send.at[q], g1_recv)
    g1_recv[my_q] = g1_send[my_q]

    for fetch in fetches[1:]:
        fetch.wait()
    weight_f32 = jnp.concatenate(
        [
            weight_ref[...].astype(jnp.float32),
            jnp.zeros((8 - weight_ref.shape[0], weight_ref.shape[1]), jnp.float32),
        ],
        axis=0,
    )
    weight_rows = weight_f32.astype(jnp.bfloat16)
    weight_cols = (
        jnp.concatenate([weight_f32, jnp.zeros_like(weight_f32)], axis=0)
        .T.astype(jnp.bfloat16)
    )
    chan = lax.broadcasted_iota(jnp.int32, (8, TILE), 0)

    def gather_two():
        plane_arrive(0, g1_recv)
        for i in range(images):
            at = i % IMG_ROW * 9
            g2_send[i // IMG_ROW, at : at + 9, :] = jnp.where(
                rank_ref[i] == 0, g1_recv[holder_q[i], 0:9], g1_recv[holder_q[i], 9:18]
            )
        line_send(0, lambda g: g2_send.at[g // 2], g2_recv)
        g2_recv[my_g] = g2_send[my_x]

    def gather_three():
        line_arrive(0, g2_recv)
        for i in range(IMG_ROW):
            at = i * 9
            g3_send[at : at + 9, :] = g2_recv[
                holder_g[my_x * IMG_ROW + i], at : at + 9
            ]
        plane_send(1, lambda q: g3_send, g3_recv)
        g3_recv[my_q] = g3_send[...]

    def splat_tile(t):
        px = pl.ds(pl.multiple_of(t * TILE, TILE), TILE)
        cell = spread(cell_ref[pl.ds(pl.multiple_of(t * 8, 8), 8), :])
        cx = cell >> 7
        cy = (cell >> 3) & (GY - 1)
        cz = cell & (GZ - 1)
        fx = jnp.broadcast_to(frac_ref[0:1, px], (8, TILE))
        fy = jnp.broadcast_to(frac_ref[1:2, px], (8, TILE))
        fz = jnp.broadcast_to(frac_ref[2:3, px], (8, TILE))
        az = hat(cz, chan, 1.0 - fz, fz)
        gy = 1.0 - fy
        for y in range(0, GY, 2):
            pair = jnp.concatenate(
                [hat(cy, y, gy, fy) * az, hat(cy, y + 1, gy, fy) * az], axis=0
            )
            big = pair.astype(jnp.bfloat16)
            rest = (pair - big.astype(jnp.float32)).astype(jnp.bfloat16)
            splat_ref[t, y * GZ : (y + 2) * GZ, :] = big
            splat_ref[t, YZ + y * GZ : YZ + (y + 2) * GZ, :] = rest
        gx = 1.0 - fx
        ax = jnp.concatenate([hat(cx, chan, gx, fx), hat(cx, chan + 8, gx, fx)], axis=0)
        logits = jnp.dot(
            weight_rows, feat_ref[:, px], preferred_element_type=jnp.float32
        )
        bias = jnp.where(
            chan == 0, bias_ref[0], jnp.where(chan == 1, bias_ref[1], bias_ref[2])
        )
        colour = 1.0 / (1.0 + jnp.exp(-(logits + bias)))
        colour_ref[t] = colour
        parts = []
        for k in range(3):
            u = jnp.broadcast_to(cot_ref[k : k + 1, px].astype(jnp.float32), (GX, TILE))
            uax = u * ax
            uax_ref[t, k * GX : (k + 1) * GX, :] = uax
            for j in range(3):
                col = jnp.broadcast_to(colour[j : j + 1, :], (GX, TILE))
                parts.append((uax * col).astype(jnp.bfloat16))
            parts.append(uax.astype(jnp.bfloat16))
        left = jnp.concatenate(parts, axis=0)
        both = lax.dot_general(
            left, splat_ref[t], NT, preferred_element_type=jnp.float32
        )
        grads = both[:, :YZ] + both[:, YZ:]
        image = tile_ref[t]
        for i in range(IMG_ROW):
            acc_ref[i] += jnp.where(image == i, grads, 0.0)

    def slice_tile(t):
        px = slice(t * TILE, (t + 1) * TILE)
        wide = jnp.dot(
            grid_ref[tile_ref[t]], splat_ref[t], preferred_element_type=jnp.float32
        )
        d_colour = jnp.zeros((8, TILE), jnp.float32)
        for j in range(3):
            total = None
            for k in range(3):
                at = (3 * k + j) * GX
                coef = wide[at : at + GX] + wide[USED + at : USED + at + GX]
                term = coef * uax_ref[t, k * GX : (k + 1) * GX, :]
                total = term if total is None else total + term
            whole = jnp.sum(total, axis=0, keepdims=True)
            d_colour = jnp.where(chan == j, whole, d_colour)
        colour = colour_ref[t]
        d_logits = d_colour * colour * (1.0 - colour)
        d_half = jnp.concatenate([d_logits, jnp.zeros_like(d_logits)], axis=0).astype(
            jnp.bfloat16
        )
        half_ref[:, px] = d_half
        return sum(d_logits[:, n : n + 128] for n in range(0, TILE, 128))

    def run(body, unroll):
        def step(n, carry):
            for m in range(unroll):
                body(unroll * n + m)
            return carry

        lax.fori_loop(0, tiles // unroll, step, 0)

    run(splat_tile, SPLAT_UNROLL)

    sibling = pltpu.make_async_remote_copy(
        src_ref=acc_ref.at[pl.ds(2 * (1 - my_c), 2)],
        dst_ref=sib_ref,
        send_sem=sib_sems.at[0],
        recv_sem=sib_sems.at[1],
        device_id={"img": my_x, "pix": my_q * 2 + 1 - my_c},
        device_id_type=MESH,
    )
    sibling.start()
    gather_two()
    sibling.wait()
    for i in range(2):
        total_ref[i] = acc_ref[2 * my_c + i] + sib_ref[i]
    for q in range(planes):
        for i in range(2):
            r1_send[q, i * COEF : (i + 1) * COEF, :] = total_ref[
                i, pl.ds(q, COEF, stride=GX), :
            ]
    plane_send(2, lambda q: r1_send.at[q], r1_recv)
    r1_recv[my_q] = r1_send[my_q]

    gather_three()

    def find_dest(q, carry):
        dev = my_x * (planes * 2) + q * 2 + my_c
        for s in range(OWN_MOST):
            found = jnp.int32(images)
            for i in range(images):
                found = jnp.where((holders[i] == dev) & (ranks[i] == s), i, found)
            dest_ref[q * OWN_MOST + s] = found
        return carry

    lax.fori_loop(0, planes, find_dest, 0)

    def turn_tile(t):
        px = pl.ds(pl.multiple_of(t * TILE, TILE), TILE)
        feat_t_ref[px, :] = feat_ref[:, px].T

    def reduce_two():
        plane_arrive(2, r1_recv)
        total = r1_recv[0]
        for q in range(1, planes):
            total = total + r1_recv[q]
        for i in range(2):
            r2_send[i] = total[i * COEF : (i + 1) * COEF]
        line_send(1, lambda g: r2_send, r2_recv)
        r2_recv[my_g] = r2_send[...]
        r2_recv[groups] = jnp.zeros_like(r2_send)

    def reduce_three():
        line_arrive(1, r2_recv)
        for q in range(planes):
            for s in range(OWN_MOST):
                i = dest_ref[q * OWN_MOST + s]
                r3_send[q, s] = r2_recv[i // 2, i % 2]
        plane_send(3, lambda q: r3_send.at[q], r3_recv)
        r3_recv[my_q] = r3_send[my_q]

    reduce_two()

    lane = lax.broadcasted_iota(jnp.int32, (COEF, YZ), 1)
    for s in range(OWN_MOST):
        own = [
            table_ref[q, pl.ds(own_row[s], COEF, stride=held), :]
            for q in range(planes)
        ]
        for q in range(planes):
            here = own[q]
            total = jnp.zeros((COEF, YZ), jnp.float32)
            if q > 0:
                total = total + (here - own[q - 1])
            if q < planes - 1:
                total = total - (own[q + 1] - here)
            for step, first, last in (
                (GZ, lane >= GZ, lane < YZ - GZ),
                (1, lane % GZ != 0, lane % GZ != GZ - 1),
            ):
                before = jnp.where(first, here - pltpu.roll(here, step, 1), 0.0)
                after = jnp.where(last, pltpu.roll(here, YZ - step, 1) - here, 0.0)
                total = total + (before - after)
            tv_ref[q, s] = jnp.where(own_has[s] == 1, total, 0.0)

    run(turn_tile, 8)
    for q in [my_q] + plane_q[::-1]:
        if q is not my_q:
            plane_copy(1, q, g3_recv.at[q], g3_recv.at[q], q).wait_recv()
        for i in range(IMG_ROW):
            grid_f32[i, pl.ds(q, 9, stride=GX), :] = g3_recv[q, i * 9 : (i + 1) * 9]
    for i in range(IMG_ROW):
        full = grid_f32[i]
        big = full.astype(jnp.bfloat16)
        rest = (full - big.astype(jnp.float32)).astype(jnp.bfloat16)
        grid_ref[i, 0:USED, 0:YZ] = big
        grid_ref[i, 0:USED, YZ : 2 * YZ] = big
        grid_ref[i, USED : 2 * USED, 0:YZ] = rest
        grid_ref[i, USED : 2 * USED, YZ : 2 * YZ] = rest

    bias_part = sum(slice_tile(t) for t in range(tiles))

    head = jnp.dot(
        half_ref[...], feat_t_ref[...], preferred_element_type=jnp.float32
    )
    bias_sum = jnp.sum(bias_part, axis=1, keepdims=True)
    on_row = lax.broadcasted_iota(jnp.int32, (8, head.shape[1]), 0)
    on_lane = lax.broadcasted_iota(jnp.int32, (8, head.shape[1]), 1)
    bias_row = jnp.sum(
        jnp.where(on_row == on_lane, bias_sum, 0.0), axis=0, keepdims=True
    )
    stat_ref[0:1, :] = jnp.concatenate([head[0:1], head[1:2]], axis=1)
    stat_ref[1:2, :] = jnp.concatenate([head[2:3], bias_row], axis=1)
    own_stat = pltpu.make_async_copy(stat_ref, h1_recv.at[my_dev], head_sems.at[1])
    own_stat.start()
    for dev in head_devs:
        head_copy(dev).start()
    reduce_three()

    def feature_tile(t):
        px = pl.ds(pl.multiple_of(t * TILE, TILE), TILE)
        fgrad_ref[:, px] = jnp.dot(
            weight_cols, half_ref[:, px], preferred_element_type=jnp.float32
        ).astype(jnp.bfloat16)

    run(feature_tile, FEATURE_UNROLL)
    plane_arrive(3, r3_recv)
    for q in range(planes):
        for s in range(OWN_MOST):
            owned_ref[:, s, q * YZ : (q + 1) * YZ] = r3_recv[q, s] + tv_ref[q, s]
    for q in plane_q:
        plane_copy(0, q, g1_send.at[q], g1_recv.at[my_q]).wait_send()
        plane_copy(1, q, g3_send, g3_recv.at[my_q]).wait_send()
        plane_copy(2, q, r1_send.at[q], r1_recv.at[my_q]).wait_send()
        plane_copy(3, q, r3_send.at[q], r3_recv.at[my_q]).wait_send()
    for g in line_g:
        line_copy(0, g, g2_send.at[g // 2], g2_recv.at[my_g]).wait_send()
        line_copy(1, g, r2_send, r2_recv.at[my_g]).wait_send()

    pltpu.make_async_copy(h1_recv, h1_recv, head_sems.at[1]).wait()
    count = h1_recv.shape[0]
    sums = [
        jnp.sum(h1_recv[n : n + count // 8], axis=0) for n in range(0, count, count // 8)
    ]
    while len(sums) > 1:
        sums = [a + b for a, b in zip(sums[::2], sums[1::2])]
    head_ref[...] = sums[0]
    sent = h1_recv.at[pl.ds(0, len(head_devs))]
    pltpu.make_async_copy(sent, sent, head_sems.at[0]).wait()


def finish(
    owned_in,
    stat_in,
    fgrad_in,
    owned_out,
    head_out,
    bias_out,
    fgrad_out,
    head_ref,
    bias_ref,
    sems,
):
    parts = 4
    rows = fgrad_in.shape[0] // parts
    copies = [
        (fgrad_in.at[pl.ds(n * rows, rows)], fgrad_out.at[pl.ds(n * rows, rows)])
        for n in range(parts)
    ]
    copies += [(owned_in, owned_out), (head_ref, head_out), (bias_ref, bias_out)]
    copies = [
        pltpu.make_async_copy(src, dst, sems.at[n])
        for n, (src, dst) in enumerate(copies)
    ]
    for copy in copies[:-2]:
        copy.start()
    width = head_ref.shape[1]
    head_ref[0:1, :] = stat_in[0:1, 0:width]
    head_ref[1:2, :] = stat_in[0:1, width : 2 * width]
    head_ref[2:3, :] = stat_in[1:2, 0:width]
    bias_ref[...] = stat_in[1, width : width + bias_ref.shape[0]]
    for copy in copies[-2:]:
        copy.start()
    for copy in copies:
        copy.wait()


def shards(side, rows_x, ids, table, tile_image, cell, frac, feat, weight, bias, cot):
    pixels = cell.shape[0]
    tiles = pixels // TILE
    planes = side * side
    groups = rows_x * 2
    images = ids.shape[0]
    f32, bf16, i32 = jnp.float32, jnp.bfloat16, jnp.int32
    chunk = (COEF, YZ)
    vmem = pl.BlockSpec(memory_space=pltpu.VMEM)
    hbm = pl.BlockSpec(memory_space=pltpu.HBM)
    table_rows = jnp.transpose(table, (1, 0, 2)).reshape(-1, CELLS)
    cell_rows = cell.reshape(pixels // 128, 128)
    owned, stat, fgrad = pl.pallas_call(
        functools.partial(kernel, side, rows_x),
        out_shape=(
            jax.ShapeDtypeStruct((COEF, OWN_MOST, CELLS), f32),
            jax.ShapeDtypeStruct((2, 128), f32),
            jax.ShapeDtypeStruct(feat.shape, bf16),
        ),
        in_specs=[hbm] * 9,
        out_specs=(vmem, vmem, vmem),
        scratch_shapes=[
            pltpu.SMEM(ids.shape, i32),
            pltpu.SMEM(tile_image.shape, i32),
            pltpu.SMEM(bias.shape, f32),
            pltpu.VMEM((planes, table_rows.shape[0], YZ), f32),
            pltpu.VMEM(cell_rows.shape, i32),
            pltpu.VMEM(frac.shape, f32),
            pltpu.VMEM(feat.shape, bf16),
            pltpu.VMEM(weight.shape, bf16),
            pltpu.VMEM(cot.shape, bf16),
            pltpu.SemaphoreType.DMA((8 + planes,)),
            pltpu.VMEM((tiles, 2 * YZ, TILE), bf16),
            pltpu.VMEM((tiles, 3 * GX, TILE), f32),
            pltpu.VMEM((tiles, 8, TILE), f32),
            pltpu.VMEM((16, pixels), bf16),
            pltpu.VMEM((pixels, feat.shape[0]), bf16),
            pltpu.VMEM((IMG_ROW, ROWS, YZ), f32),
            pltpu.VMEM((2, ROWS, YZ), f32),
            pltpu.VMEM((2, ROWS, YZ), f32),
            pltpu.VMEM((IMG_ROW, USED, YZ), f32),
            pltpu.VMEM((IMG_ROW, 2 * USED, 2 * YZ), bf16),
            pltpu.VMEM((planes, OWN_MOST) + chunk, f32),
            pltpu.VMEM((2, 128), f32),
            pltpu.SMEM((images,), i32),
            pltpu.SMEM((images,), i32),
            pltpu.SMEM((images,), i32),
            pltpu.SMEM((planes * OWN_MOST,), i32),
            pltpu.VMEM((planes, OWN_MOST * 9, YZ), f32),
            pltpu.VMEM((planes, OWN_MOST * 9, YZ), f32),
            pltpu.VMEM((rows_x, IMG_ROW * 9, YZ), f32),
            pltpu.VMEM((groups, IMG_ROW * 9, YZ), f32),
            pltpu.VMEM((IMG_ROW * 9, YZ), f32),
            pltpu.VMEM((planes, IMG_ROW * 9, YZ), f32),
            pltpu.VMEM((planes, 2 * COEF, YZ), f32),
            pltpu.VMEM((planes, 2 * COEF, YZ), f32),
            pltpu.VMEM((2,) + chunk, f32),
            pltpu.VMEM((groups + 1, 2) + chunk, f32),
            pltpu.VMEM((planes, OWN_MOST) + chunk, f32),
            pltpu.VMEM((planes, OWN_MOST) + chunk, f32),
            pltpu.VMEM((planes * groups, 2, 128), f32),
            pltpu.SemaphoreType.DMA((2,)),
            pltpu.SemaphoreType.DMA((2,)),
            pltpu.SemaphoreType.DMA((4, planes)),
            pltpu.SemaphoreType.DMA((4, planes)),
            pltpu.SemaphoreType.DMA((2, groups)),
            pltpu.SemaphoreType.DMA((2, groups)),
        ],
        compiler_params=pltpu.CompilerParams(
            collective_id=0, has_side_effects=True, vmem_limit_bytes=VMEM_LIMIT
        ),
    )(
        *(
            pltpu.with_memory_space_constraint(operand, pltpu.HBM)
            for operand in (
                ids,
                tile_image,
                bias,
                table_rows,
                cell_rows,
                frac,
                feat,
                weight,
                cot,
            )
        )
    )
    owned, head, bias_grad, fgrad = pl.pallas_call(
        finish,
        out_shape=(
            jax.ShapeDtypeStruct((COEF, OWN_MOST, CELLS), f32),
            jax.ShapeDtypeStruct(weight.shape, f32),
            jax.ShapeDtypeStruct(bias.shape, f32),
            jax.ShapeDtypeStruct(feat.shape, bf16),
        ),
        in_specs=[vmem, vmem, vmem],
        out_specs=(hbm, hbm, hbm, hbm),
        scratch_shapes=[
            pltpu.VMEM(weight.shape, f32),
            pltpu.VMEM(bias.shape, f32),
            pltpu.SemaphoreType.DMA((7,)),
        ],
        compiler_params=pltpu.CompilerParams(vmem_limit_bytes=16 << 20),
    )(owned, stat, fgrad)
    return jnp.transpose(owned, (1, 0, 2)), head, bias_grad, fgrad


def solution(mesh):
    rows_x = mesh.shape["img"]
    side = math.isqrt(mesh.shape["pix"] // 2)
    return jax.shard_map(
        functools.partial(shards, side, rows_x),
        mesh=mesh,
        in_specs=(
            P(),
            P(("img", "pix"), None, None),
            P(("img", "pix")),
            P(("img", "pix")),
            P(None, ("img", "pix")),
            P(None, ("img", "pix")),
            P(),
            P(),
            P(None, ("img", "pix")),
        ),
        out_specs=(P(("img", "pix"), None, None), P(), P(), P(None, ("img", "pix"))),
        check_vma=False,
    )
```

```python
import functools
import math

import jax
import jax.numpy as jnp
from jax import lax
from jax.experimental import pallas as pl
from jax.experimental.pallas import tpu as pltpu
from jax.sharding import PartitionSpec as P

GX = 16
GY = 16
GZ = 8
YZ = GY * GZ
CELLS = GX * YZ
COEF = 12
TILE = 1024
IMG_ROW = 4
OWN_MOST = 2
ROWS = COEF * GX
USED = 9 * GX
VMEM_LIMIT = 40 << 20
SPLAT_UNROLL = 16
FEATURE_UNROLL = 8
MESH = pl.DeviceIdType.MESH
NT = (((1,), (1,)), ((), ()))


def spread(block):
    return jnp.concatenate(
        [jnp.broadcast_to(block[s : s + 1, :], (8, 128)) for s in range(8)], axis=1
    )


def hat(coord, level, low, high):
    return jnp.where(coord == level, low, jnp.where(coord == level - 1, high, 0.0))


def hops(a, b):
    return min(a % b, -a % b)


def kernel(
    side,
    rows_x,
    ids_any,
    tile_any,
    bias_any,
    table_any,
    cell_any,
    frac_any,
    feat_any,
    weight_any,
    cot_any,
    owned_ref,
    head_ref,
    fgrad_ref,
    ids_ref,
    tile_ref,
    bias_ref,
    table_ref,
    cell_ref,
    frac_ref,
    feat_ref,
    weight_ref,
    cot_ref,
    in_sems,
    splat_ref,
    uax_ref,
    colour_ref,
    half_ref,
    feat_t_ref,
    acc_ref,
    sib_ref,
    total_ref,
    grid_f32,
    grid_ref,
    tv_ref,
    stat_ref,
    holder_q,
    holder_g,
    rank_ref,
    dest_ref,
    g1_send,
    g1_recv,
    g2_send,
    g2_recv,
    g3_send,
    g3_recv,
    r1_send,
    r1_recv,
    r2_send,
    r2_recv,
    r3_send,
    r3_recv,
    h1_recv,
    head_sems,
    sib_sems,
    plane_ss,
    plane_rs,
    line_ss,
    line_rs,
):
    operands = (
        (ids_any, ids_ref),
        (cell_any, cell_ref),
        (frac_any, frac_ref),
        (feat_any, feat_ref),
        (weight_any, weight_ref),
        (cot_any, cot_ref),
        (tile_any, tile_ref),
        (bias_any, bias_ref),
    )
    fetches = [
        pltpu.make_async_copy(src, dst, in_sems.at[n])
        for n, (src, dst) in enumerate(operands)
    ]
    planes = side * side
    table_fetches = [
        pltpu.make_async_copy(
            table_any.at[:, pl.ds(q * YZ, YZ)],
            table_ref.at[q, pl.ds(0, table_any.shape[0])],
            in_sems.at[len(operands) + q],
        )
        for q in range(planes)
    ]
    groups = rows_x * 2
    tiles = cell_ref.shape[0] // 8
    images = ids_ref.shape[0]
    held = table_any.shape[0] // COEF
    my_x = lax.axis_index("img")
    my_pix = lax.axis_index("pix")
    my_q = my_pix // 2
    my_c = my_pix % 2
    my_g = my_x * 2 + my_c
    my_dev = my_x * (planes * 2) + my_pix

    steps = [(dz, dy) for dz in range(side) for dy in range(side)]
    steps = sorted(steps, key=lambda d: -hops(d[0], side) - hops(d[1], side))[:-1]
    my_z, my_y = my_q // side, my_q % side
    plane_q = [(my_z + dz) % side * side + (my_y + dy) % side for dz, dy in steps]
    steps = [(dx, dc) for dx in range(rows_x) for dc in range(2)]
    steps = sorted(steps, key=lambda d: -2 * hops(d[0], rows_x) - d[1])[:-1]
    line_g = [(my_x + dx) % rows_x * 2 + (my_c + dc) % 2 for dx, dc in steps]

    def plane_dev(q):
        return {"img": my_x, "pix": q * 2 + my_c}

    def line_dev(g):
        return {"img": g // 2, "pix": my_q * 2 + g % 2}

    def plane_copy(stage, q, src, dst, slot=None):
        return pltpu.make_async_remote_copy(
            src_ref=src,
            dst_ref=dst,
            send_sem=plane_ss.at[stage, q],
            recv_sem=plane_rs.at[stage, my_q if slot is None else slot],
            device_id=plane_dev(q),
            device_id_type=MESH,
        )

    def line_copy(stage, g, src, dst, slot=None):
        return pltpu.make_async_remote_copy(
            src_ref=src,
            dst_ref=dst,
            send_sem=line_ss.at[stage, g],
            recv_sem=line_rs.at[stage, my_g if slot is None else slot],
            device_id=line_dev(g),
            device_id_type=MESH,
        )

    steps = [
        (dx, dz, dy, dc)
        for dx in range(rows_x)
        for dz in range(side)
        for dy in range(side)
        for dc in range(2)
    ]
    far = [hops(dx, rows_x) + hops(dz, side) + hops(dy, side) for dx, dz, dy, _ in steps]
    order = sorted(range(len(steps)), key=lambda n: -2 * far[n] - steps[n][3])[:-1]
    head_devs = []
    for dx, dz, dy, dc in [steps[n] for n in order]:
        q = (my_z + dz) % side * side + (my_y + dy) % side
        head_devs.append(
            {"img": (my_x + dx) % rows_x, "pix": q * 2 + (my_c + dc) % 2}
        )

    def head_copy(dev):
        return pltpu.make_async_remote_copy(
            src_ref=stat_ref,
            dst_ref=h1_recv.at[my_dev],
            send_sem=head_sems.at[0],
            recv_sem=head_sems.at[1],
            device_id=dev,
            device_id_type=MESH,
        )

    def plane_send(stage, src, dst):
        for q in plane_q:
            plane_copy(stage, q, src(q), dst.at[my_q]).start()

    def line_send(stage, src, dst):
        for g in line_g:
            line_copy(stage, g, src(g), dst.at[my_g]).start()

    def plane_arrive(stage, buf):
        for q in plane_q:
            plane_copy(stage, q, buf.at[q], buf.at[q], q).wait_recv()

    def line_arrive(stage, buf):
        for g in line_g:
            line_copy(stage, g, buf.at[g], buf.at[g], g).wait_recv()

    barrier = pltpu.get_barrier_semaphore()
    for q in plane_q:
        pl.semaphore_signal(
            barrier, inc=1, device_id=plane_dev(q), device_id_type=MESH
        )
    for g in line_g:
        pl.semaphore_signal(barrier, inc=1, device_id=line_dev(g), device_id_type=MESH)

    for fetch in fetches[:1] + table_fetches + fetches[1:]:
        fetch.start()

    acc_ref[...] = jnp.zeros_like(acc_ref)
    fetches[0].wait()
    holders = []
    ranks = []
    for i in range(images):
        holder = ids_ref[i] // held
        rank = jnp.int32(0)
        for other in holders:
            rank = rank + jnp.where(other == holder, 1, 0)
        holders.append(holder)
        ranks.append(rank)
        hp = holder % (planes * 2)
        holder_q[i] = hp // 2
        holder_g[i] = holder // (planes * 2) * 2 + hp % 2
        rank_ref[i] = rank

    own_row = [jnp.int32(0)] * OWN_MOST
    own_has = [jnp.int32(0)] * OWN_MOST
    for i in range(images):
        for s in range(OWN_MOST):
            hit = (holders[i] == my_dev) & (ranks[i] == s)
            own_row[s] = jnp.where(hit, ids_ref[i] % held, own_row[s])
            own_has[s] = jnp.where(hit, 1, own_has[s])

    for fetch in table_fetches:
        fetch.wait()
    for s in range(OWN_MOST):
        for q in range(planes):
            for k in range(3):
                g1_send[q, s * 9 + 3 * k : s * 9 + 3 * k + 3, :] = table_ref[
                    q, pl.ds(4 * k * held + own_row[s], 3, stride=held), :
                ]
    pl.semaphore_wait(barrier, len(plane_q) + len(line_g))
    plane_send(0, lambda q: g1_send.at[q], g1_recv)
    g1_recv[my_q] = g1_send[my_q]

    for fetch in fetches[1:]:
        fetch.wait()
    weight_f32 = jnp.concatenate(
        [
            weight_ref[...].astype(jnp.float32),
            jnp.zeros((8 - weight_ref.shape[0], weight_ref.shape[1]), jnp.float32),
        ],
        axis=0,
    )
    weight_rows = weight_f32.astype(jnp.bfloat16)
    weight_cols = (
        jnp.concatenate([weight_f32, jnp.zeros_like(weight_f32)], axis=0)
        .T.astype(jnp.bfloat16)
    )
    chan = lax.broadcasted_iota(jnp.int32, (8, TILE), 0)

    def gather_two():
        plane_arrive(0, g1_recv)
        for i in range(images):
            at = i % IMG_ROW * 9
            g2_send[i // IMG_ROW, at : at + 9, :] = jnp.where(
                rank_ref[i] == 0, g1_recv[holder_q[i], 0:9], g1_recv[holder_q[i], 9:18]
            )
        line_send(0, lambda g: g2_send.at[g // 2], g2_recv)
        g2_recv[my_g] = g2_send[my_x]

    def gather_three():
        line_arrive(0, g2_recv)
        for i in range(IMG_ROW):
            at = i * 9
            g3_send[0, at : at + 9, :] = g2_recv[
                holder_g[my_x * IMG_ROW + i], at : at + 9
            ]
        plane_send(1, lambda q: g3_send.at[0], g3_recv)
        g3_recv[my_q] = g3_send[0]

    def splat_tile(t):
        px = pl.ds(pl.multiple_of(t * TILE, TILE), TILE)
        cell = spread(cell_ref[pl.ds(pl.multiple_of(t * 8, 8), 8), :])
        cx = cell >> 7
        cy = (cell >> 3) & (GY - 1)
        cz = cell & (GZ - 1)
        fx = jnp.broadcast_to(frac_ref[0:1, px], (8, TILE))
        fy = jnp.broadcast_to(frac_ref[1:2, px], (8, TILE))
        fz = jnp.broadcast_to(frac_ref[2:3, px], (8, TILE))
        az = hat(cz, chan, 1.0 - fz, fz)
        gy = 1.0 - fy
        for y in range(0, GY, 2):
            pair = jnp.concatenate(
                [hat(cy, y, gy, fy) * az, hat(cy, y + 1, gy, fy) * az], axis=0
            )
            big = pair.astype(jnp.bfloat16)
            rest = (pair - big.astype(jnp.float32)).astype(jnp.bfloat16)
            splat_ref[t, y * GZ : (y + 2) * GZ, :] = big
            splat_ref[t, YZ + y * GZ : YZ + (y + 2) * GZ, :] = rest
        gx = 1.0 - fx
        ax = jnp.concatenate([hat(cx, chan, gx, fx), hat(cx, chan + 8, gx, fx)], axis=0)
        logits = jnp.dot(
            weight_rows, feat_ref[:, px], preferred_element_type=jnp.float32
        )
        bias = jnp.where(
            chan == 0, bias_ref[0], jnp.where(chan == 1, bias_ref[1], bias_ref[2])
        )
        colour = 1.0 / (1.0 + jnp.exp(-(logits + bias)))
        colour_ref[t] = colour
        parts = []
        for k in range(3):
            u = jnp.broadcast_to(cot_ref[k : k + 1, px].astype(jnp.float32), (GX, TILE))
            uax = u * ax
            uax_ref[t, k * GX : (k + 1) * GX, :] = uax
            for j in range(3):
                col = jnp.broadcast_to(colour[j : j + 1, :], (GX, TILE))
                parts.append((uax * col).astype(jnp.bfloat16))
            parts.append(uax.astype(jnp.bfloat16))
        left = jnp.concatenate(parts, axis=0)
        both = lax.dot_general(
            left, splat_ref[t], NT, preferred_element_type=jnp.float32
        )
        grads = both[:, :YZ] + both[:, YZ:]
        image = tile_ref[t]
        for i in range(IMG_ROW):
            acc_ref[i] += jnp.where(image == i, grads, 0.0)

    def slice_tile(t):
        px = slice(t * TILE, (t + 1) * TILE)
        wide = jnp.dot(
            grid_ref[tile_ref[t]], splat_ref[t], preferred_element_type=jnp.float32
        )
        d_colour = jnp.zeros((8, TILE), jnp.float32)
        for j in range(3):
            total = None
            for k in range(3):
                at = (3 * k + j) * GX
                coef = wide[at : at + GX] + wide[USED + at : USED + at + GX]
                term = coef * uax_ref[t, k * GX : (k + 1) * GX, :]
                total = term if total is None else total + term
            whole = jnp.sum(total, axis=0, keepdims=True)
            d_colour = jnp.where(chan == j, whole, d_colour)
        colour = colour_ref[t]
        d_logits = d_colour * colour * (1.0 - colour)
        d_half = jnp.concatenate([d_logits, jnp.zeros_like(d_logits)], axis=0).astype(
            jnp.bfloat16
        )
        half_ref[:, px] = d_half
        return sum(d_logits[:, n : n + 128] for n in range(0, TILE, 128))

    def run(body, unroll):
        def step(n, carry):
            for m in range(unroll):
                body(unroll * n + m)
            return carry

        lax.fori_loop(0, tiles // unroll, step, 0)

    run(splat_tile, SPLAT_UNROLL)

    sibling = pltpu.make_async_remote_copy(
        src_ref=acc_ref.at[pl.ds(2 * (1 - my_c), 2)],
        dst_ref=sib_ref,
        send_sem=sib_sems.at[0],
        recv_sem=sib_sems.at[1],
        device_id={"img": my_x, "pix": my_q * 2 + 1 - my_c},
        device_id_type=MESH,
    )
    sibling.start()
    gather_two()
    sibling.wait()
    for i in range(2):
        total_ref[i, 0:ROWS] = acc_ref[2 * my_c + i] + sib_ref[i]
    for q in range(planes):
        for i in range(2):
            r1_send[q, i * COEF : (i + 1) * COEF, :] = total_ref[
                i, pl.ds(q, COEF, stride=GX), :
            ]
    plane_send(2, lambda q: r1_send.at[q], r1_recv)
    r1_recv[my_q] = r1_send[my_q]

    gather_three()

    def find_dest(q, carry):
        dev = my_x * (planes * 2) + q * 2 + my_c
        for s in range(OWN_MOST):
            found = jnp.int32(images)
            for i in range(images):
                found = jnp.where((holders[i] == dev) & (ranks[i] == s), i, found)
            dest_ref[q * OWN_MOST + s] = found
        return carry

    lax.fori_loop(0, planes, find_dest, 0)

    def turn_tile(t):
        px = pl.ds(pl.multiple_of(t * TILE, TILE), TILE)
        feat_t_ref[px, :] = feat_ref[:, px].T

    def reduce_two():
        plane_arrive(2, r1_recv)
        total = r1_recv[0]
        for q in range(1, planes):
            total = total + r1_recv[q]
        for i in range(2):
            r2_send[i] = total[i * COEF : (i + 1) * COEF]
        line_send(1, lambda g: r2_send, r2_recv)
        r2_recv[my_g] = r2_send[...]
        r2_recv[groups] = jnp.zeros_like(r2_send)

    def reduce_three():
        line_arrive(1, r2_recv)
        for q in range(planes):
            for s in range(OWN_MOST):
                i = dest_ref[q * OWN_MOST + s]
                r3_send[q, s] = r2_recv[i // 2, i % 2]
        plane_send(3, lambda q: r3_send.at[q], r3_recv)
        r3_recv[my_q] = r3_send[my_q]

    reduce_two()

    lane = lax.broadcasted_iota(jnp.int32, (COEF, YZ), 1)
    for s in range(OWN_MOST):
        own = [
            table_ref[q, pl.ds(own_row[s], COEF, stride=held), :]
            for q in range(planes)
        ]
        for q in range(planes):
            here = own[q]
            total = jnp.zeros((COEF, YZ), jnp.float32)
            if q > 0:
                total = total + (here - own[q - 1])
            if q < planes - 1:
                total = total - (own[q + 1] - here)
            for step, first, last in (
                (GZ, lane >= GZ, lane < YZ - GZ),
                (1, lane % GZ != 0, lane % GZ != GZ - 1),
            ):
                before = jnp.where(first, here - pltpu.roll(here, step, 1), 0.0)
                after = jnp.where(last, pltpu.roll(here, YZ - step, 1) - here, 0.0)
                total = total + (before - after)
            tv_ref[q, s] = jnp.where(own_has[s] == 1, total, 0.0)

    run(turn_tile, 8)
    for q in [my_q] + plane_q[::-1]:
        if q is not my_q:
            plane_copy(1, q, g3_recv.at[q], g3_recv.at[q], q).wait_recv()
        for i in range(IMG_ROW):
            grid_f32[i, pl.ds(q, 9, stride=GX), :] = g3_recv[q, i * 9 : (i + 1) * 9]
    for i in range(IMG_ROW):
        full = grid_f32[i, 0:USED]
        big = full.astype(jnp.bfloat16)
        rest = (full - big.astype(jnp.float32)).astype(jnp.bfloat16)
        grid_ref[i, 0:USED, 0:YZ] = big
        grid_ref[i, 0:USED, YZ : 2 * YZ] = big
        grid_ref[i, USED : 2 * USED, 0:YZ] = rest
        grid_ref[i, USED : 2 * USED, YZ : 2 * YZ] = rest

    bias_part = sum(slice_tile(t) for t in range(tiles))

    head = jnp.dot(
        half_ref[...], feat_t_ref[...], preferred_element_type=jnp.float32
    )
    bias_sum = jnp.sum(bias_part, axis=1, keepdims=True)
    on_row = lax.broadcasted_iota(jnp.int32, (8, head.shape[1]), 0)
    on_lane = lax.broadcasted_iota(jnp.int32, (8, head.shape[1]), 1)
    bias_row = jnp.sum(
        jnp.where(on_row == on_lane, bias_sum, 0.0), axis=0, keepdims=True
    )
    stat_ref[0:1, :] = jnp.concatenate([head[0:1], head[1:2]], axis=1)
    stat_ref[1:2, :] = jnp.concatenate([head[2:3], bias_row], axis=1)
    own_stat = pltpu.make_async_copy(stat_ref, h1_recv.at[my_dev], head_sems.at[1])
    own_stat.start()
    for dev in head_devs:
        head_copy(dev).start()
    reduce_three()

    def feature_tile(t):
        px = pl.ds(pl.multiple_of(t * TILE, TILE), TILE)
        fgrad_ref[:, px] = jnp.dot(
            weight_cols, half_ref[:, px], preferred_element_type=jnp.float32
        ).astype(jnp.bfloat16)

    run(feature_tile, FEATURE_UNROLL)
    plane_arrive(3, r3_recv)
    for q in range(planes):
        for s in range(OWN_MOST):
            owned_ref[:, s, q * YZ : (q + 1) * YZ] = r3_recv[q, s] + tv_ref[q, s]
    for q in plane_q:
        plane_copy(0, q, g1_send.at[q], g1_recv.at[my_q]).wait_send()
        plane_copy(1, q, g3_send.at[0], g3_recv.at[my_q]).wait_send()
        plane_copy(2, q, r1_send.at[q], r1_recv.at[my_q]).wait_send()
        plane_copy(3, q, r3_send.at[q], r3_recv.at[my_q]).wait_send()
    for g in line_g:
        line_copy(0, g, g2_send.at[g // 2], g2_recv.at[my_g]).wait_send()
        line_copy(1, g, r2_send, r2_recv.at[my_g]).wait_send()

    pltpu.make_async_copy(h1_recv, h1_recv, head_sems.at[1]).wait()
    count = h1_recv.shape[0]
    sums = [
        jnp.sum(h1_recv[n : n + count // 8], axis=0) for n in range(0, count, count // 8)
    ]
    while len(sums) > 1:
        sums = [a + b for a, b in zip(sums[::2], sums[1::2])]
    head_ref[...] = sums[0]
    sent = h1_recv.at[pl.ds(0, len(head_devs))]
    pltpu.make_async_copy(sent, sent, head_sems.at[0]).wait()


def finish(
    owned_in,
    stat_in,
    fgrad_in,
    owned_out,
    head_out,
    bias_out,
    fgrad_out,
    head_ref,
    bias_ref,
    sems,
):
    parts = 4
    rows = fgrad_in.shape[0] // parts
    copies = [
        (fgrad_in.at[pl.ds(n * rows, rows)], fgrad_out.at[pl.ds(n * rows, rows)])
        for n in range(parts)
    ]
    copies += [(owned_in, owned_out), (head_ref, head_out), (bias_ref, bias_out)]
    copies = [
        pltpu.make_async_copy(src, dst, sems.at[n])
        for n, (src, dst) in enumerate(copies)
    ]
    for copy in copies[:-2]:
        copy.start()
    width = head_ref.shape[1]
    head_ref[0:1, :] = stat_in[0:1, 0:width]
    head_ref[1:2, :] = stat_in[0:1, width : 2 * width]
    head_ref[2:3, :] = stat_in[1:2, 0:width]
    bias_ref[...] = stat_in[1, width : width + bias_ref.shape[0]]
    for copy in copies[-2:]:
        copy.start()
    for copy in copies:
        copy.wait()


def shards(side, rows_x, ids, table, tile_image, cell, frac, feat, weight, bias, cot):
    pixels = cell.shape[0]
    tiles = pixels // TILE
    planes = side * side
    groups = rows_x * 2
    images = ids.shape[0]
    f32, bf16, i32 = jnp.float32, jnp.bfloat16, jnp.int32
    chunk = (COEF, YZ)
    vmem = pl.BlockSpec(memory_space=pltpu.VMEM)
    hbm = pl.BlockSpec(memory_space=pltpu.HBM)
    table_rows = jnp.transpose(table, (1, 0, 2)).reshape(-1, CELLS)
    cell_rows = cell.reshape(pixels // 128, 128)
    owned, stat, fgrad = pl.pallas_call(
        functools.partial(kernel, side, rows_x),
        out_shape=(
            jax.ShapeDtypeStruct((COEF, OWN_MOST, CELLS), f32),
            jax.ShapeDtypeStruct((2, 128), f32),
            jax.ShapeDtypeStruct(feat.shape, bf16),
        ),
        in_specs=[hbm] * 9,
        out_specs=(vmem, vmem, vmem),
        scratch_shapes=[
            pltpu.SMEM(ids.shape, i32),
            pltpu.SMEM(tile_image.shape, i32),
            pltpu.SMEM(bias.shape, f32),
            pltpu.VMEM((planes, table_rows.shape[0] * 16 // COEF, YZ), f32),
            pltpu.VMEM(cell_rows.shape, i32),
            pltpu.VMEM(frac.shape, f32),
            pltpu.VMEM(feat.shape, bf16),
            pltpu.VMEM(weight.shape, bf16),
            pltpu.VMEM(cot.shape, bf16),
            pltpu.SemaphoreType.DMA((8 + planes,)),
            pltpu.VMEM((tiles, 2 * YZ, TILE), bf16),
            pltpu.VMEM((tiles, 3 * GX, TILE), f32),
            pltpu.VMEM((tiles, 8, TILE), f32),
            pltpu.VMEM((16, pixels), bf16),
            pltpu.VMEM((pixels, feat.shape[0]), bf16),
            pltpu.VMEM((IMG_ROW, ROWS, YZ), f32),
            pltpu.VMEM((2, ROWS, YZ), f32),
            pltpu.VMEM((2, 16 * GX, YZ), f32),
            pltpu.VMEM((IMG_ROW, 16 * GX, YZ), f32),
            pltpu.VMEM((IMG_ROW, 2 * USED, 2 * YZ), bf16),
            pltpu.VMEM((planes, OWN_MOST) + chunk, f32),
            pltpu.VMEM((2, 128), f32),
            pltpu.SMEM((images,), i32),
            pltpu.SMEM((images,), i32),
            pltpu.SMEM((images,), i32),
            pltpu.SMEM((planes * OWN_MOST,), i32),
            pltpu.VMEM((planes + 1, OWN_MOST * 9, YZ), f32),
            pltpu.VMEM((planes + 1, OWN_MOST * 9, YZ), f32),
            pltpu.VMEM((rows_x + 1, IMG_ROW * 9, YZ), f32),
            pltpu.VMEM((groups + 1, IMG_ROW * 9, YZ), f32),
            pltpu.VMEM((2, IMG_ROW * 9, YZ), f32),
            pltpu.VMEM((planes + 1, IMG_ROW * 9, YZ), f32),
            pltpu.VMEM((planes + 1, 2 * COEF, YZ), f32),
            pltpu.VMEM((planes + 1, 2 * COEF, YZ), f32),
            pltpu.VMEM((2,) + chunk, f32),
            pltpu.VMEM((groups + 1, 2) + chunk, f32),
            pltpu.VMEM((planes, OWN_MOST) + chunk, f32),
            pltpu.VMEM((planes, OWN_MOST) + chunk, f32),
            pltpu.VMEM((planes * groups, 2, 128), f32),
            pltpu.SemaphoreType.DMA((2,)),
            pltpu.SemaphoreType.DMA((2,)),
            pltpu.SemaphoreType.DMA((4, planes)),
            pltpu.SemaphoreType.DMA((4, planes)),
            pltpu.SemaphoreType.DMA((2, groups)),
            pltpu.SemaphoreType.DMA((2, groups)),
        ],
        compiler_params=pltpu.CompilerParams(
            collective_id=0, has_side_effects=True, vmem_limit_bytes=VMEM_LIMIT
        ),
    )(
        *(
            pltpu.with_memory_space_constraint(operand, pltpu.HBM)
            for operand in (
                ids,
                tile_image,
                bias,
                table_rows,
                cell_rows,
                frac,
                feat,
                weight,
                cot,
            )
        )
    )
    owned, head, bias_grad, fgrad = pl.pallas_call(
        finish,
        out_shape=(
            jax.ShapeDtypeStruct((COEF, OWN_MOST, CELLS), f32),
            jax.ShapeDtypeStruct(weight.shape, f32),
            jax.ShapeDtypeStruct(bias.shape, f32),
            jax.ShapeDtypeStruct(feat.shape, bf16),
        ),
        in_specs=[vmem, vmem, vmem],
        out_specs=(hbm, hbm, hbm, hbm),
        scratch_shapes=[
            pltpu.VMEM(weight.shape, f32),
            pltpu.VMEM(bias.shape, f32),
            pltpu.SemaphoreType.DMA((7,)),
        ],
        compiler_params=pltpu.CompilerParams(vmem_limit_bytes=16 << 20),
    )(owned, stat, fgrad)
    return jnp.transpose(owned, (1, 0, 2)), head, bias_grad, fgrad


def solution(mesh):
    rows_x = mesh.shape["img"]
    side = math.isqrt(mesh.shape["pix"] // 2)
    return jax.shard_map(
        functools.partial(shards, side, rows_x),
        mesh=mesh,
        in_specs=(
            P(),
            P(("img", "pix"), None, None),
            P(("img", "pix")),
            P(("img", "pix")),
            P(None, ("img", "pix")),
            P(None, ("img", "pix")),
            P(),
            P(),
            P(None, ("img", "pix")),
        ),
        out_specs=(P(("img", "pix"), None, None), P(), P(), P(None, ("img", "pix"))),
        check_vma=False,
    )
```

```python
import functools
import math

import jax
import jax.numpy as jnp
from jax import lax
from jax.experimental import pallas as pl
from jax.experimental.pallas import tpu as pltpu
from jax.sharding import PartitionSpec as P

GX = 16
GY = 16
GZ = 8
YZ = GY * GZ
CELLS = GX * YZ
COEF = 12
TILE = 1024
IMG_ROW = 4
OWN_MOST = 2
ROWS = COEF * GX
USED = 9 * GX
VMEM_LIMIT = 40 << 20
SPLAT_UNROLL = 16
FEATURE_UNROLL = 8
MESH = pl.DeviceIdType.MESH
NT = (((1,), (1,)), ((), ()))


def spread(block):
    return jnp.concatenate(
        [jnp.broadcast_to(block[s : s + 1, :], (8, 128)) for s in range(8)], axis=1
    )


def hat(coord, level, low, high):
    return jnp.where(coord == level, low, jnp.where(coord == level - 1, high, 0.0))


def hops(a, b):
    return min(a % b, -a % b)


def kernel(
    side,
    rows_x,
    ids_any,
    tile_any,
    bias_any,
    table_any,
    cell_any,
    frac_any,
    feat_any,
    weight_any,
    cot_any,
    owned_ref,
    head_ref,
    fgrad_ref,
    ids_ref,
    tile_ref,
    bias_ref,
    table_ref,
    cell_ref,
    frac_ref,
    feat_ref,
    weight_ref,
    cot_ref,
    in_sems,
    splat_ref,
    uax_ref,
    colour_ref,
    half_ref,
    feat_t_ref,
    acc_ref,
    sib_ref,
    total_ref,
    grid_f32,
    grid_ref,
    tv_ref,
    stat_ref,
    holder_q,
    holder_g,
    rank_ref,
    dest_ref,
    g1_send,
    g1_recv,
    g2_send,
    g2_recv,
    g3_send,
    g3_recv,
    r1_send,
    r1_recv,
    r2_send,
    r2_recv,
    r3_send,
    r3_recv,
    h1_recv,
    head_sems,
    sib_sems,
    plane_ss,
    plane_rs,
    line_ss,
    line_rs,
):
    operands = (
        (ids_any, ids_ref),
        (cell_any, cell_ref),
        (frac_any, frac_ref),
        (feat_any, feat_ref),
        (weight_any, weight_ref),
        (cot_any, cot_ref),
        (tile_any, tile_ref),
        (bias_any, bias_ref),
    )
    fetches = [
        pltpu.make_async_copy(src, dst, in_sems.at[n])
        for n, (src, dst) in enumerate(operands)
    ]
    planes = side * side
    table_fetches = [
        pltpu.make_async_copy(
            table_any.at[:, pl.ds(q * YZ, YZ)],
            table_ref.at[q, pl.ds(0, table_any.shape[0])],
            in_sems.at[len(operands) + q],
        )
        for q in range(planes)
    ]
    groups = rows_x * 2
    tiles = cell_ref.shape[0] // 8
    images = ids_ref.shape[0]
    held = table_any.shape[0] // COEF
    my_x = lax.axis_index("img")
    my_pix = lax.axis_index("pix")
    my_q = my_pix // 2
    my_c = my_pix % 2
    my_g = my_x * 2 + my_c
    my_dev = my_x * (planes * 2) + my_pix

    steps = [(dz, dy) for dz in range(side) for dy in range(side)]
    steps = sorted(steps, key=lambda d: -hops(d[0], side) - hops(d[1], side))[:-1]
    my_z, my_y = my_q // side, my_q % side
    plane_q = [(my_z + dz) % side * side + (my_y + dy) % side for dz, dy in steps]
    steps = [(dx, dc) for dx in range(rows_x) for dc in range(2)]
    steps = sorted(steps, key=lambda d: -2 * hops(d[0], rows_x) - d[1])[:-1]
    line_g = [(my_x + dx) % rows_x * 2 + (my_c + dc) % 2 for dx, dc in steps]

    def plane_dev(q):
        return {"img": my_x, "pix": q * 2 + my_c}

    def line_dev(g):
        return {"img": g // 2, "pix": my_q * 2 + g % 2}

    def plane_copy(stage, q, src, dst, slot=None):
        return pltpu.make_async_remote_copy(
            src_ref=src,
            dst_ref=dst,
            send_sem=plane_ss.at[stage, q],
            recv_sem=plane_rs.at[stage, my_q if slot is None else slot],
            device_id=plane_dev(q),
            device_id_type=MESH,
        )

    def line_copy(stage, g, src, dst, slot=None):
        return pltpu.make_async_remote_copy(
            src_ref=src,
            dst_ref=dst,
            send_sem=line_ss.at[stage, g],
            recv_sem=line_rs.at[stage, my_g if slot is None else slot],
            device_id=line_dev(g),
            device_id_type=MESH,
        )

    steps = [
        (dx, dz, dy, dc)
        for dx in range(rows_x)
        for dz in range(side)
        for dy in range(side)
        for dc in range(2)
    ]
    far = [hops(dx, rows_x) + hops(dz, side) + hops(dy, side) for dx, dz, dy, _ in steps]
    order = sorted(range(len(steps)), key=lambda n: -2 * far[n] - steps[n][3])[:-1]
    head_devs = []
    for dx, dz, dy, dc in [steps[n] for n in order]:
        q = (my_z + dz) % side * side + (my_y + dy) % side
        head_devs.append(
            {"img": (my_x + dx) % rows_x, "pix": q * 2 + (my_c + dc) % 2}
        )

    def head_copy(dev):
        return pltpu.make_async_remote_copy(
            src_ref=stat_ref,
            dst_ref=h1_recv.at[my_dev],
            send_sem=head_sems.at[0],
            recv_sem=head_sems.at[1],
            device_id=dev,
            device_id_type=MESH,
        )

    def plane_send(stage, src, dst):
        for q in plane_q:
            plane_copy(stage, q, src(q), dst.at[my_q]).start()

    def line_send(stage, src, dst):
        for g in line_g:
            line_copy(stage, g, src(g), dst.at[my_g]).start()

    def plane_arrive(stage, buf):
        for q in plane_q:
            plane_copy(stage, q, buf.at[q], buf.at[q], q).wait_recv()

    def line_arrive(stage, buf):
        for g in line_g:
            line_copy(stage, g, buf.at[g], buf.at[g], g).wait_recv()

    barrier = pltpu.get_barrier_semaphore()
    for q in plane_q:
        pl.semaphore_signal(
            barrier, inc=1, device_id=plane_dev(q), device_id_type=MESH
        )
    for g in line_g:
        pl.semaphore_signal(barrier, inc=1, device_id=line_dev(g), device_id_type=MESH)

    for fetch in fetches[:1] + table_fetches + fetches[1:]:
        fetch.start()

    acc_ref[...] = jnp.zeros_like(acc_ref)
    fetches[0].wait()
    holders = []
    ranks = []
    for i in range(images):
        holder = ids_ref[i] // held
        rank = jnp.int32(0)
        for other in holders:
            rank = rank + jnp.where(other == holder, 1, 0)
        holders.append(holder)
        ranks.append(rank)
        hp = holder % (planes * 2)
        holder_q[i] = hp // 2
        holder_g[i] = holder // (planes * 2) * 2 + hp % 2
        rank_ref[i] = rank

    own_row = [jnp.int32(0)] * OWN_MOST
    own_has = [jnp.int32(0)] * OWN_MOST
    for i in range(images):
        for s in range(OWN_MOST):
            hit = (holders[i] == my_dev) & (ranks[i] == s)
            own_row[s] = jnp.where(hit, ids_ref[i] % held, own_row[s])
            own_has[s] = jnp.where(hit, 1, own_has[s])

    for fetch in table_fetches:
        fetch.wait()
    for s in range(OWN_MOST):
        for q in range(planes):
            for k in range(3):
                g1_send[q, s * 9 + 3 * k : s * 9 + 3 * k + 3, :] = table_ref[
                    q, pl.ds(4 * k * held + own_row[s], 3, stride=held), :
                ]
    pl.semaphore_wait(barrier, len(plane_q) + len(line_g))
    plane_send(0, lambda q: g1_send.at[q], g1_recv)
    g1_recv[my_q] = g1_send[my_q]

    for fetch in fetches[1:]:
        fetch.wait()
    weight_f32 = jnp.concatenate(
        [
            weight_ref[...].astype(jnp.float32),
            jnp.zeros((8 - weight_ref.shape[0], weight_ref.shape[1]), jnp.float32),
        ],
        axis=0,
    )
    weight_rows = weight_f32.astype(jnp.bfloat16)
    weight_cols = (
        jnp.concatenate([weight_f32, jnp.zeros_like(weight_f32)], axis=0)
        .T.astype(jnp.bfloat16)
    )
    chan = lax.broadcasted_iota(jnp.int32, (8, TILE), 0)

    def gather_two():
        plane_arrive(0, g1_recv)
        for i in range(images):
            at = i % IMG_ROW * 9
            g2_send[i // IMG_ROW, at : at + 9, :] = jnp.where(
                rank_ref[i] == 0, g1_recv[holder_q[i], 0:9], g1_recv[holder_q[i], 9:18]
            )
        line_send(0, lambda g: g2_send.at[g // 2], g2_recv)
        g2_recv[my_g] = g2_send[my_x]

    def gather_three():
        line_arrive(0, g2_recv)
        for i in range(IMG_ROW):
            at = i * 9
            g3_send[0, at : at + 9, :] = g2_recv[
                holder_g[my_x * IMG_ROW + i], at : at + 9
            ]
        plane_send(1, lambda q: g3_send.at[0], g3_recv)
        g3_recv[my_q] = g3_send[0]

    def splat_tile(t):
        px = pl.ds(pl.multiple_of(t * TILE, TILE), TILE)
        cell = spread(cell_ref[pl.ds(pl.multiple_of(t * 8, 8), 8), :])
        cx = cell >> 7
        cy = (cell >> 3) & (GY - 1)
        cz = cell & (GZ - 1)
        fx = jnp.broadcast_to(frac_ref[0:1, px], (8, TILE))
        fy = jnp.broadcast_to(frac_ref[1:2, px], (8, TILE))
        fz = jnp.broadcast_to(frac_ref[2:3, px], (8, TILE))
        az = hat(cz, chan, 1.0 - fz, fz)
        gy = 1.0 - fy
        for y in range(0, GY, 2):
            pair = jnp.concatenate(
                [hat(cy, y, gy, fy) * az, hat(cy, y + 1, gy, fy) * az], axis=0
            )
            big = pair.astype(jnp.bfloat16)
            rest = (pair - big.astype(jnp.float32)).astype(jnp.bfloat16)
            splat_ref[t, y * GZ : (y + 2) * GZ, :] = big
            splat_ref[t, YZ + y * GZ : YZ + (y + 2) * GZ, :] = rest
        gx = 1.0 - fx
        ax = jnp.concatenate([hat(cx, chan, gx, fx), hat(cx, chan + 8, gx, fx)], axis=0)
        logits = jnp.dot(
            weight_rows, feat_ref[:, px], preferred_element_type=jnp.float32
        )
        bias = jnp.where(
            chan == 0, bias_ref[0], jnp.where(chan == 1, bias_ref[1], bias_ref[2])
        )
        colour = 1.0 / (1.0 + jnp.exp(-(logits + bias)))
        colour_ref[t] = colour
        parts = []
        for k in range(3):
            u = jnp.broadcast_to(cot_ref[k : k + 1, px].astype(jnp.float32), (GX, TILE))
            uax = u * ax
            uax_ref[t, k * GX : (k + 1) * GX, :] = uax
            for j in range(3):
                col = jnp.broadcast_to(colour[j : j + 1, :], (GX, TILE))
                parts.append((uax * col).astype(jnp.bfloat16))
            parts.append(uax.astype(jnp.bfloat16))
        left = jnp.concatenate(parts, axis=0)
        both = lax.dot_general(
            left, splat_ref[t], NT, preferred_element_type=jnp.float32
        )
        grads = both[:, :YZ] + both[:, YZ:]
        image = tile_ref[t]
        for i in range(IMG_ROW):
            acc_ref[i] += jnp.where(image == i, grads, 0.0)

    def slice_tile(t):
        px = slice(t * TILE, (t + 1) * TILE)
        wide = jnp.dot(
            grid_ref[tile_ref[t]], splat_ref[t], preferred_element_type=jnp.float32
        )
        d_colour = jnp.zeros((8, TILE), jnp.float32)
        for j in range(3):
            total = None
            for k in range(3):
                at = (3 * k + j) * GX
                coef = wide[at : at + GX] + wide[USED + at : USED + at + GX]
                term = coef * uax_ref[t, k * GX : (k + 1) * GX, :]
                total = term if total is None else total + term
            whole = jnp.sum(total, axis=0, keepdims=True)
            d_colour = jnp.where(chan == j, whole, d_colour)
        colour = colour_ref[t]
        d_logits = d_colour * colour * (1.0 - colour)
        d_half = jnp.concatenate([d_logits, jnp.zeros_like(d_logits)], axis=0).astype(
            jnp.bfloat16
        )
        half_ref[:, px] = d_half
        return sum(d_logits[:, n : n + 128] for n in range(0, TILE, 128))

    def run(body, unroll):
        def step(n, carry):
            for m in range(unroll):
                body(unroll * n + m)
            return carry

        lax.fori_loop(0, tiles // unroll, step, 0)

    run(splat_tile, SPLAT_UNROLL)

    sibling = pltpu.make_async_remote_copy(
        src_ref=acc_ref.at[pl.ds(2 * (1 - my_c), 2)],
        dst_ref=sib_ref,
        send_sem=sib_sems.at[0],
        recv_sem=sib_sems.at[1],
        device_id={"img": my_x, "pix": my_q * 2 + 1 - my_c},
        device_id_type=MESH,
    )
    sibling.start()
    gather_two()
    sibling.wait()
    for i in range(2):
        total_ref[i, 0:ROWS] = acc_ref[2 * my_c + i] + sib_ref[i]
    for q in range(planes):
        for i in range(2):
            r1_send[q, i * COEF : (i + 1) * COEF, :] = total_ref[
                i, pl.ds(q, COEF, stride=GX), :
            ]
    plane_send(2, lambda q: r1_send.at[q], r1_recv)
    r1_recv[my_q] = r1_send[my_q]

    gather_three()

    def turn_tile(t):
        px = pl.ds(pl.multiple_of(t * TILE, TILE), TILE)
        feat_t_ref[px, :] = feat_ref[:, px].T

    def reduce_two():
        plane_arrive(2, r1_recv)
        total = r1_recv[0]
        for q in range(1, planes):
            total = total + r1_recv[q]
        for i in range(2):
            r2_send[i] = total[i * COEF : (i + 1) * COEF]
        line_send(1, lambda g: r2_send, r2_recv)
        r2_recv[my_g] = r2_send[...]
        r2_recv[groups] = jnp.zeros_like(r2_send)

    def reduce_three():
        line_arrive(1, r2_recv)
        for q in range(planes):
            for s in range(OWN_MOST):
                i = dest_ref[q * OWN_MOST + s]
                r3_send[q, s] = r2_recv[i // 2, i % 2]
        plane_send(3, lambda q: r3_send.at[q], r3_recv)
        r3_recv[my_q] = r3_send[my_q]

    reduce_two()

    def find_dest(q, carry):
        dev = my_x * (planes * 2) + q * 2 + my_c
        for s in range(OWN_MOST):
            found = jnp.int32(images)
            for i in range(images):
                found = jnp.where((holders[i] == dev) & (ranks[i] == s), i, found)
            dest_ref[q * OWN_MOST + s] = found
        return carry

    lax.fori_loop(0, planes, find_dest, 0)


    lane = lax.broadcasted_iota(jnp.int32, (COEF, YZ), 1)
    for s in range(OWN_MOST):
        own = [
            table_ref[q, pl.ds(own_row[s], COEF, stride=held), :]
            for q in range(planes)
        ]
        for q in range(planes):
            here = own[q]
            total = jnp.zeros((COEF, YZ), jnp.float32)
            if q > 0:
                total = total + (here - own[q - 1])
            if q < planes - 1:
                total = total - (own[q + 1] - here)
            for step, first, last in (
                (GZ, lane >= GZ, lane < YZ - GZ),
                (1, lane % GZ != 0, lane % GZ != GZ - 1),
            ):
                before = jnp.where(first, here - pltpu.roll(here, step, 1), 0.0)
                after = jnp.where(last, pltpu.roll(here, YZ - step, 1) - here, 0.0)
                total = total + (before - after)
            tv_ref[q, s] = jnp.where(own_has[s] == 1, total, 0.0)

    run(turn_tile, 8)
    for q in [my_q] + plane_q[::-1]:
        if q is not my_q:
            plane_copy(1, q, g3_recv.at[q], g3_recv.at[q], q).wait_recv()
        for i in range(IMG_ROW):
            grid_f32[i, pl.ds(q, 9, stride=GX), :] = g3_recv[q, i * 9 : (i + 1) * 9]
    for i in range(IMG_ROW):
        full = grid_f32[i, 0:USED]
        big = full.astype(jnp.bfloat16)
        rest = (full - big.astype(jnp.float32)).astype(jnp.bfloat16)
        grid_ref[i, 0:USED, 0:YZ] = big
        grid_ref[i, 0:USED, YZ : 2 * YZ] = big
        grid_ref[i, USED : 2 * USED, 0:YZ] = rest
        grid_ref[i, USED : 2 * USED, YZ : 2 * YZ] = rest

    bias_part = sum(slice_tile(t) for t in range(tiles))

    head = jnp.dot(
        half_ref[...], feat_t_ref[...], preferred_element_type=jnp.float32
    )
    bias_sum = jnp.sum(bias_part, axis=1, keepdims=True)
    on_row = lax.broadcasted_iota(jnp.int32, (8, head.shape[1]), 0)
    on_lane = lax.broadcasted_iota(jnp.int32, (8, head.shape[1]), 1)
    bias_row = jnp.sum(
        jnp.where(on_row == on_lane, bias_sum, 0.0), axis=0, keepdims=True
    )
    stat_ref[0:1, :] = jnp.concatenate([head[0:1], head[1:2]], axis=1)
    stat_ref[1:2, :] = jnp.concatenate([head[2:3], bias_row], axis=1)
    own_stat = pltpu.make_async_copy(stat_ref, h1_recv.at[my_dev], head_sems.at[1])
    own_stat.start()
    for dev in head_devs:
        head_copy(dev).start()
    reduce_three()

    def feature_tile(t):
        px = pl.ds(pl.multiple_of(t * TILE, TILE), TILE)
        fgrad_ref[:, px] = jnp.dot(
            weight_cols, half_ref[:, px], preferred_element_type=jnp.float32
        ).astype(jnp.bfloat16)

    run(feature_tile, FEATURE_UNROLL)
    plane_arrive(3, r3_recv)
    for q in range(planes):
        for s in range(OWN_MOST):
            owned_ref[:, s, q * YZ : (q + 1) * YZ] = r3_recv[q, s] + tv_ref[q, s]
    for q in plane_q:
        plane_copy(0, q, g1_send.at[q], g1_recv.at[my_q]).wait_send()
        plane_copy(1, q, g3_send.at[0], g3_recv.at[my_q]).wait_send()
        plane_copy(2, q, r1_send.at[q], r1_recv.at[my_q]).wait_send()
        plane_copy(3, q, r3_send.at[q], r3_recv.at[my_q]).wait_send()
    for g in line_g:
        line_copy(0, g, g2_send.at[g // 2], g2_recv.at[my_g]).wait_send()
        line_copy(1, g, r2_send, r2_recv.at[my_g]).wait_send()

    pltpu.make_async_copy(h1_recv, h1_recv, head_sems.at[1]).wait()
    count = h1_recv.shape[0]
    sums = [
        jnp.sum(h1_recv[n : n + count // 8], axis=0) for n in range(0, count, count // 8)
    ]
    while len(sums) > 1:
        sums = [a + b for a, b in zip(sums[::2], sums[1::2])]
    head_ref[...] = sums[0]
    sent = h1_recv.at[pl.ds(0, len(head_devs))]
    pltpu.make_async_copy(sent, sent, head_sems.at[0]).wait()


def finish(
    owned_in,
    stat_in,
    fgrad_in,
    owned_out,
    head_out,
    bias_out,
    fgrad_out,
    head_ref,
    bias_ref,
    sems,
):
    parts = 4
    rows = fgrad_in.shape[0] // parts
    copies = [
        (fgrad_in.at[pl.ds(n * rows, rows)], fgrad_out.at[pl.ds(n * rows, rows)])
        for n in range(parts)
    ]
    copies += [(owned_in, owned_out), (head_ref, head_out), (bias_ref, bias_out)]
    copies = [
        pltpu.make_async_copy(src, dst, sems.at[n])
        for n, (src, dst) in enumerate(copies)
    ]
    for copy in copies[:-2]:
        copy.start()
    width = head_ref.shape[1]
    head_ref[0:1, :] = stat_in[0:1, 0:width]
    head_ref[1:2, :] = stat_in[0:1, width : 2 * width]
    head_ref[2:3, :] = stat_in[1:2, 0:width]
    bias_ref[...] = stat_in[1, width : width + bias_ref.shape[0]]
    for copy in copies[-2:]:
        copy.start()
    for copy in copies:
        copy.wait()


def shards(side, rows_x, ids, table, tile_image, cell, frac, feat, weight, bias, cot):
    pixels = cell.shape[0]
    tiles = pixels // TILE
    planes = side * side
    groups = rows_x * 2
    images = ids.shape[0]
    f32, bf16, i32 = jnp.float32, jnp.bfloat16, jnp.int32
    chunk = (COEF, YZ)
    vmem = pl.BlockSpec(memory_space=pltpu.VMEM)
    hbm = pl.BlockSpec(memory_space=pltpu.HBM)
    table_rows = jnp.transpose(table, (1, 0, 2)).reshape(-1, CELLS)
    cell_rows = cell.reshape(pixels // 128, 128)
    owned, stat, fgrad = pl.pallas_call(
        functools.partial(kernel, side, rows_x),
        out_shape=(
            jax.ShapeDtypeStruct((COEF, OWN_MOST, CELLS), f32),
            jax.ShapeDtypeStruct((2, 128), f32),
            jax.ShapeDtypeStruct(feat.shape, bf16),
        ),
        in_specs=[hbm] * 9,
        out_specs=(vmem, vmem, vmem),
        scratch_shapes=[
            pltpu.SMEM(ids.shape, i32),
            pltpu.SMEM(tile_image.shape, i32),
            pltpu.SMEM(bias.shape, f32),
            pltpu.VMEM((planes, table_rows.shape[0] * 16 // COEF, YZ), f32),
            pltpu.VMEM(cell_rows.shape, i32),
            pltpu.VMEM(frac.shape, f32),
            pltpu.VMEM(feat.shape, bf16),
            pltpu.VMEM(weight.shape, bf16),
            pltpu.VMEM(cot.shape, bf16),
            pltpu.SemaphoreType.DMA((8 + planes,)),
            pltpu.VMEM((tiles, 2 * YZ, TILE), bf16),
            pltpu.VMEM((tiles, 3 * GX, TILE), f32),
            pltpu.VMEM((tiles, 8, TILE), f32),
            pltpu.VMEM((16, pixels), bf16),
            pltpu.VMEM((pixels, feat.shape[0]), bf16),
            pltpu.VMEM((IMG_ROW, ROWS, YZ), f32),
            pltpu.VMEM((2, ROWS, YZ), f32),
            pltpu.VMEM((2, 16 * GX, YZ), f32),
            pltpu.VMEM((IMG_ROW, 16 * GX, YZ), f32),
            pltpu.VMEM((IMG_ROW, 2 * USED, 2 * YZ), bf16),
            pltpu.VMEM((planes, OWN_MOST) + chunk, f32),
            pltpu.VMEM((2, 128), f32),
            pltpu.SMEM((images,), i32),
            pltpu.SMEM((images,), i32),
            pltpu.SMEM((images,), i32),
            pltpu.SMEM((planes * OWN_MOST,), i32),
            pltpu.VMEM((planes + 1, OWN_MOST * 9, YZ), f32),
            pltpu.VMEM((planes + 1, OWN_MOST * 9, YZ), f32),
            pltpu.VMEM((rows_x + 1, IMG_ROW * 9, YZ), f32),
            pltpu.VMEM((groups + 1, IMG_ROW * 9, YZ), f32),
            pltpu.VMEM((2, IMG_ROW * 9, YZ), f32),
            pltpu.VMEM((planes + 1, IMG_ROW * 9, YZ), f32),
            pltpu.VMEM((planes + 1, 2 * COEF, YZ), f32),
            pltpu.VMEM((planes + 1, 2 * COEF, YZ), f32),
            pltpu.VMEM((2,) + chunk, f32),
            pltpu.VMEM((groups + 1, 2) + chunk, f32),
            pltpu.VMEM((planes, OWN_MOST) + chunk, f32),
            pltpu.VMEM((planes, OWN_MOST) + chunk, f32),
            pltpu.VMEM((planes * groups, 2, 128), f32),
            pltpu.SemaphoreType.DMA((2,)),
            pltpu.SemaphoreType.DMA((2,)),
            pltpu.SemaphoreType.DMA((4, planes)),
            pltpu.SemaphoreType.DMA((4, planes)),
            pltpu.SemaphoreType.DMA((2, groups)),
            pltpu.SemaphoreType.DMA((2, groups)),
        ],
        compiler_params=pltpu.CompilerParams(
            collective_id=0, has_side_effects=True, vmem_limit_bytes=VMEM_LIMIT
        ),
    )(
        *(
            pltpu.with_memory_space_constraint(operand, pltpu.HBM)
            for operand in (
                ids,
                tile_image,
                bias,
                table_rows,
                cell_rows,
                frac,
                feat,
                weight,
                cot,
            )
        )
    )
    owned, head, bias_grad, fgrad = pl.pallas_call(
        finish,
        out_shape=(
            jax.ShapeDtypeStruct((COEF, OWN_MOST, CELLS), f32),
            jax.ShapeDtypeStruct(weight.shape, f32),
            jax.ShapeDtypeStruct(bias.shape, f32),
            jax.ShapeDtypeStruct(feat.shape, bf16),
        ),
        in_specs=[vmem, vmem, vmem],
        out_specs=(hbm, hbm, hbm, hbm),
        scratch_shapes=[
            pltpu.VMEM(weight.shape, f32),
            pltpu.VMEM(bias.shape, f32),
            pltpu.SemaphoreType.DMA((7,)),
        ],
        compiler_params=pltpu.CompilerParams(vmem_limit_bytes=16 << 20),
    )(owned, stat, fgrad)
    return jnp.transpose(owned, (1, 0, 2)), head, bias_grad, fgrad


def solution(mesh):
    rows_x = mesh.shape["img"]
    side = math.isqrt(mesh.shape["pix"] // 2)
    return jax.shard_map(
        functools.partial(shards, side, rows_x),
        mesh=mesh,
        in_specs=(
            P(),
            P(("img", "pix"), None, None),
            P(("img", "pix")),
            P(("img", "pix")),
            P(None, ("img", "pix")),
            P(None, ("img", "pix")),
            P(),
            P(),
            P(None, ("img", "pix")),
        ),
        out_specs=(P(("img", "pix"), None, None), P(), P(), P(None, ("img", "pix"))),
        check_vma=False,
    )
```

```python
import functools
import math

import jax
import jax.numpy as jnp
from jax import lax
from jax.experimental import pallas as pl
from jax.experimental.pallas import tpu as pltpu
from jax.sharding import PartitionSpec as P

GX = 16
GY = 16
GZ = 8
YZ = GY * GZ
CELLS = GX * YZ
COEF = 12
TILE = 1024
IMG_ROW = 4
OWN_MOST = 2
ROWS = COEF * GX
USED = 9 * GX
VMEM_LIMIT = 40 << 20
SPLAT_UNROLL = 16
FEATURE_UNROLL = 16
MESH = pl.DeviceIdType.MESH
NT = (((1,), (1,)), ((), ()))


def spread(block):
    return jnp.concatenate(
        [jnp.broadcast_to(block[s : s + 1, :], (8, 128)) for s in range(8)], axis=1
    )


def hat(coord, level, low, high):
    return jnp.where(coord == level, low, jnp.where(coord == level - 1, high, 0.0))


def hops(a, b):
    return min(a % b, -a % b)


def kernel(
    side,
    rows_x,
    ids_any,
    tile_any,
    bias_any,
    table_any,
    cell_any,
    frac_any,
    feat_any,
    weight_any,
    cot_any,
    owned_ref,
    head_ref,
    fgrad_ref,
    ids_ref,
    tile_ref,
    bias_ref,
    table_ref,
    cell_ref,
    frac_ref,
    feat_ref,
    weight_ref,
    cot_ref,
    in_sems,
    splat_ref,
    uax_ref,
    colour_ref,
    half_ref,
    feat_t_ref,
    acc_ref,
    sib_ref,
    total_ref,
    grid_f32,
    grid_ref,
    tv_ref,
    stat_ref,
    holder_q,
    holder_g,
    rank_ref,
    dest_ref,
    g1_send,
    g1_recv,
    g2_send,
    g2_recv,
    g3_send,
    g3_recv,
    r1_send,
    r1_recv,
    r2_send,
    r2_recv,
    r3_send,
    r3_recv,
    h1_recv,
    head_sems,
    sib_sems,
    plane_ss,
    plane_rs,
    line_ss,
    line_rs,
):
    operands = (
        (ids_any, ids_ref),
        (cell_any, cell_ref),
        (frac_any, frac_ref),
        (feat_any, feat_ref),
        (weight_any, weight_ref),
        (cot_any, cot_ref),
        (tile_any, tile_ref),
        (bias_any, bias_ref),
    )
    fetches = [
        pltpu.make_async_copy(src, dst, in_sems.at[n])
        for n, (src, dst) in enumerate(operands)
    ]
    planes = side * side
    table_fetches = [
        pltpu.make_async_copy(
            table_any.at[:, pl.ds(q * YZ, YZ)],
            table_ref.at[q, pl.ds(0, table_any.shape[0])],
            in_sems.at[len(operands) + q],
        )
        for q in range(planes)
    ]
    groups = rows_x * 2
    tiles = cell_ref.shape[0] // 8
    images = ids_ref.shape[0]
    held = table_any.shape[0] // COEF
    my_x = lax.axis_index("img")
    my_pix = lax.axis_index("pix")
    my_q = my_pix // 2
    my_c = my_pix % 2
    my_g = my_x * 2 + my_c
    my_dev = my_x * (planes * 2) + my_pix

    steps = [(dz, dy) for dz in range(side) for dy in range(side)]
    steps = sorted(steps, key=lambda d: -hops(d[0], side) - hops(d[1], side))[:-1]
    my_z, my_y = my_q // side, my_q % side
    plane_q = [(my_z + dz) % side * side + (my_y + dy) % side for dz, dy in steps]
    steps = [(dx, dc) for dx in range(rows_x) for dc in range(2)]
    steps = sorted(steps, key=lambda d: -2 * hops(d[0], rows_x) - d[1])[:-1]
    line_g = [(my_x + dx) % rows_x * 2 + (my_c + dc) % 2 for dx, dc in steps]

    def plane_dev(q):
        return {"img": my_x, "pix": q * 2 + my_c}

    def line_dev(g):
        return {"img": g // 2, "pix": my_q * 2 + g % 2}

    def plane_copy(stage, q, src, dst, slot=None):
        return pltpu.make_async_remote_copy(
            src_ref=src,
            dst_ref=dst,
            send_sem=plane_ss.at[stage, q],
            recv_sem=plane_rs.at[stage, my_q if slot is None else slot],
            device_id=plane_dev(q),
            device_id_type=MESH,
        )

    def line_copy(stage, g, src, dst, slot=None):
        return pltpu.make_async_remote_copy(
            src_ref=src,
            dst_ref=dst,
            send_sem=line_ss.at[stage, g],
            recv_sem=line_rs.at[stage, my_g if slot is None else slot],
            device_id=line_dev(g),
            device_id_type=MESH,
        )

    steps = [
        (dx, dz, dy, dc)
        for dx in range(rows_x)
        for dz in range(side)
        for dy in range(side)
        for dc in range(2)
    ]
    far = [hops(dx, rows_x) + hops(dz, side) + hops(dy, side) for dx, dz, dy, _ in steps]
    order = sorted(range(len(steps)), key=lambda n: -2 * far[n] - steps[n][3])[:-1]
    head_devs = []
    for dx, dz, dy, dc in [steps[n] for n in order]:
        q = (my_z + dz) % side * side + (my_y + dy) % side
        head_devs.append(
            {"img": (my_x + dx) % rows_x, "pix": q * 2 + (my_c + dc) % 2}
        )

    def head_copy(dev):
        return pltpu.make_async_remote_copy(
            src_ref=stat_ref,
            dst_ref=h1_recv.at[my_dev],
            send_sem=head_sems.at[0],
            recv_sem=head_sems.at[1],
            device_id=dev,
            device_id_type=MESH,
        )

    def plane_send(stage, src, dst):
        for q in plane_q:
            plane_copy(stage, q, src(q), dst.at[my_q]).start()

    def line_send(stage, src, dst):
        for g in line_g:
            line_copy(stage, g, src(g), dst.at[my_g]).start()

    def plane_arrive(stage, buf):
        for q in plane_q:
            plane_copy(stage, q, buf.at[q], buf.at[q], q).wait_recv()

    def line_arrive(stage, buf):
        for g in line_g:
            line_copy(stage, g, buf.at[g], buf.at[g], g).wait_recv()

    barrier = pltpu.get_barrier_semaphore()
    for q in plane_q:
        pl.semaphore_signal(
            barrier, inc=1, device_id=plane_dev(q), device_id_type=MESH
        )
    for g in line_g:
        pl.semaphore_signal(barrier, inc=1, device_id=line_dev(g), device_id_type=MESH)

    for fetch in fetches[:1] + table_fetches + fetches[1:]:
        fetch.start()

    acc_ref[...] = jnp.zeros_like(acc_ref)
    fetches[0].wait()
    holders = []
    ranks = []
    for i in range(images):
        holder = ids_ref[i] // held
        rank = jnp.int32(0)
        for other in holders:
            rank = rank + jnp.where(other == holder, 1, 0)
        holders.append(holder)
        ranks.append(rank)
        hp = holder % (planes * 2)
        holder_q[i] = hp // 2
        holder_g[i] = holder // (planes * 2) * 2 + hp % 2
        rank_ref[i] = rank

    own_row = [jnp.int32(0)] * OWN_MOST
    own_has = [jnp.int32(0)] * OWN_MOST
    for i in range(images):
        for s in range(OWN_MOST):
            hit = (holders[i] == my_dev) & (ranks[i] == s)
            own_row[s] = jnp.where(hit, ids_ref[i] % held, own_row[s])
            own_has[s] = jnp.where(hit, 1, own_has[s])

    for fetch in table_fetches:
        fetch.wait()
    for s in range(OWN_MOST):
        for q in range(planes):
            for k in range(3):
                g1_send[q, s * 9 + 3 * k : s * 9 + 3 * k + 3, :] = table_ref[
                    q, pl.ds(4 * k * held + own_row[s], 3, stride=held), :
                ]
    pl.semaphore_wait(barrier, len(plane_q) + len(line_g))
    plane_send(0, lambda q: g1_send.at[q], g1_recv)
    g1_recv[my_q] = g1_send[my_q]

    for fetch in fetches[1:]:
        fetch.wait()
    weight_f32 = jnp.concatenate(
        [
            weight_ref[...].astype(jnp.float32),
            jnp.zeros((8 - weight_ref.shape[0], weight_ref.shape[1]), jnp.float32),
        ],
        axis=0,
    )
    weight_rows = weight_f32.astype(jnp.bfloat16)
    weight_cols = (
        jnp.concatenate([weight_f32, jnp.zeros_like(weight_f32)], axis=0)
        .T.astype(jnp.bfloat16)
    )
    chan = lax.broadcasted_iota(jnp.int32, (8, TILE), 0)

    def gather_two():
        plane_arrive(0, g1_recv)
        for i in range(images):
            at = i % IMG_ROW * 9
            g2_send[i // IMG_ROW, at : at + 9, :] = jnp.where(
                rank_ref[i] == 0, g1_recv[holder_q[i], 0:9], g1_recv[holder_q[i], 9:18]
            )
        line_send(0, lambda g: g2_send.at[g // 2], g2_recv)
        g2_recv[my_g] = g2_send[my_x]

    def gather_three():
        line_arrive(0, g2_recv)
        for i in range(IMG_ROW):
            at = i * 9
            g3_send[0, at : at + 9, :] = g2_recv[
                holder_g[my_x * IMG_ROW + i], at : at + 9
            ]
        plane_send(1, lambda q: g3_send.at[0], g3_recv)
        g3_recv[my_q] = g3_send[0]

    def splat_tile(t):
        px = pl.ds(pl.multiple_of(t * TILE, TILE), TILE)
        cell = spread(cell_ref[pl.ds(pl.multiple_of(t * 8, 8), 8), :])
        cx = cell >> 7
        cy = (cell >> 3) & (GY - 1)
        cz = cell & (GZ - 1)
        fx = jnp.broadcast_to(frac_ref[0:1, px], (8, TILE))
        fy = jnp.broadcast_to(frac_ref[1:2, px], (8, TILE))
        fz = jnp.broadcast_to(frac_ref[2:3, px], (8, TILE))
        az = hat(cz, chan, 1.0 - fz, fz)
        gy = 1.0 - fy
        for y in range(0, GY, 2):
            pair = jnp.concatenate(
                [hat(cy, y, gy, fy) * az, hat(cy, y + 1, gy, fy) * az], axis=0
            )
            big = pair.astype(jnp.bfloat16)
            rest = (pair - big.astype(jnp.float32)).astype(jnp.bfloat16)
            splat_ref[t, y * GZ : (y + 2) * GZ, :] = big
            splat_ref[t, YZ + y * GZ : YZ + (y + 2) * GZ, :] = rest
        gx = 1.0 - fx
        ax = jnp.concatenate([hat(cx, chan, gx, fx), hat(cx, chan + 8, gx, fx)], axis=0)
        logits = jnp.dot(
            weight_rows, feat_ref[:, px], preferred_element_type=jnp.float32
        )
        bias = jnp.where(
            chan == 0, bias_ref[0], jnp.where(chan == 1, bias_ref[1], bias_ref[2])
        )
        colour = 1.0 / (1.0 + jnp.exp(-(logits + bias)))
        colour_ref[t] = colour
        parts = []
        for k in range(3):
            u = jnp.broadcast_to(cot_ref[k : k + 1, px].astype(jnp.float32), (GX, TILE))
            uax = u * ax
            uax_ref[t, k * GX : (k + 1) * GX, :] = uax
            for j in range(3):
                col = jnp.broadcast_to(colour[j : j + 1, :], (GX, TILE))
                parts.append((uax * col).astype(jnp.bfloat16))
            parts.append(uax.astype(jnp.bfloat16))
        left = jnp.concatenate(parts, axis=0)
        both = lax.dot_general(
            left, splat_ref[t], NT, preferred_element_type=jnp.float32
        )
        grads = both[:, :YZ] + both[:, YZ:]
        image = tile_ref[t]
        for i in range(IMG_ROW):
            acc_ref[i] += jnp.where(image == i, grads, 0.0)

    def slice_tile(t):
        px = slice(t * TILE, (t + 1) * TILE)
        wide = jnp.dot(
            grid_ref[tile_ref[t]], splat_ref[t], preferred_element_type=jnp.float32
        )
        d_colour = jnp.zeros((8, TILE), jnp.float32)
        for j in range(3):
            total = None
            for k in range(3):
                at = (3 * k + j) * GX
                coef = wide[at : at + GX] + wide[USED + at : USED + at + GX]
                term = coef * uax_ref[t, k * GX : (k + 1) * GX, :]
                total = term if total is None else total + term
            whole = jnp.sum(total, axis=0, keepdims=True)
            d_colour = jnp.where(chan == j, whole, d_colour)
        colour = colour_ref[t]
        d_logits = d_colour * colour * (1.0 - colour)
        d_half = jnp.concatenate([d_logits, jnp.zeros_like(d_logits)], axis=0).astype(
            jnp.bfloat16
        )
        half_ref[:, px] = d_half
        return sum(d_logits[:, n : n + 128] for n in range(0, TILE, 128))

    def run(body, unroll):
        def step(n, carry):
            for m in range(unroll):
                body(unroll * n + m)
            return carry

        lax.fori_loop(0, tiles // unroll, step, 0)

    run(splat_tile, SPLAT_UNROLL)

    sibling = pltpu.make_async_remote_copy(
        src_ref=acc_ref.at[pl.ds(2 * (1 - my_c), 2)],
        dst_ref=sib_ref,
        send_sem=sib_sems.at[0],
        recv_sem=sib_sems.at[1],
        device_id={"img": my_x, "pix": my_q * 2 + 1 - my_c},
        device_id_type=MESH,
    )
    sibling.start()
    gather_two()
    sibling.wait()
    for i in range(2):
        total_ref[i, 0:ROWS] = acc_ref[2 * my_c + i] + sib_ref[i]
    for q in range(planes):
        for i in range(2):
            r1_send[q, i * COEF : (i + 1) * COEF, :] = total_ref[
                i, pl.ds(q, COEF, stride=GX), :
            ]
    plane_send(2, lambda q: r1_send.at[q], r1_recv)
    r1_recv[my_q] = r1_send[my_q]

    gather_three()

    def find_dest(q, carry):
        dev = my_x * (planes * 2) + q * 2 + my_c
        for s in range(OWN_MOST):
            found = jnp.int32(images)
            for i in range(images):
                found = jnp.where((holders[i] == dev) & (ranks[i] == s), i, found)
            dest_ref[q * OWN_MOST + s] = found
        return carry

    lax.fori_loop(0, planes, find_dest, 0)

    def turn_tile(t):
        px = pl.ds(pl.multiple_of(t * TILE, TILE), TILE)
        feat_t_ref[px, :] = feat_ref[:, px].T

    def reduce_two():
        plane_arrive(2, r1_recv)
        total = r1_recv[0]
        for q in range(1, planes):
            total = total + r1_recv[q]
        for i in range(2):
            r2_send[i] = total[i * COEF : (i + 1) * COEF]
        line_send(1, lambda g: r2_send, r2_recv)
        r2_recv[my_g] = r2_send[...]
        r2_recv[groups] = jnp.zeros_like(r2_send)

    def reduce_three():
        line_arrive(1, r2_recv)
        for q in range(planes):
            for s in range(OWN_MOST):
                i = dest_ref[q * OWN_MOST + s]
                r3_send[q, s] = r2_recv[i // 2, i % 2]
        plane_send(3, lambda q: r3_send.at[q], r3_recv)
        r3_recv[my_q] = r3_send[my_q]

    reduce_two()

    lane = lax.broadcasted_iota(jnp.int32, (COEF, YZ), 1)
    for s in range(OWN_MOST):
        own = [
            table_ref[q, pl.ds(own_row[s], COEF, stride=held), :]
            for q in range(planes)
        ]
        for q in range(planes):
            here = own[q]
            total = jnp.zeros((COEF, YZ), jnp.float32)
            if q > 0:
                total = total + (here - own[q - 1])
            if q < planes - 1:
                total = total - (own[q + 1] - here)
            for step, first, last in (
                (GZ, lane >= GZ, lane < YZ - GZ),
                (1, lane % GZ != 0, lane % GZ != GZ - 1),
            ):
                before = jnp.where(first, here - pltpu.roll(here, step, 1), 0.0)
                after = jnp.where(last, pltpu.roll(here, YZ - step, 1) - here, 0.0)
                total = total + (before - after)
            tv_ref[q, s] = jnp.where(own_has[s] == 1, total, 0.0)

    run(turn_tile, 8)
    for q in [my_q] + plane_q[::-1]:
        if q is not my_q:
            plane_copy(1, q, g3_recv.at[q], g3_recv.at[q], q).wait_recv()
        for i in range(IMG_ROW):
            grid_f32[i, pl.ds(q, 9, stride=GX), :] = g3_recv[q, i * 9 : (i + 1) * 9]
    for i in range(IMG_ROW):
        full = grid_f32[i, 0:USED]
        big = full.astype(jnp.bfloat16)
        rest = (full - big.astype(jnp.float32)).astype(jnp.bfloat16)
        grid_ref[i, 0:USED, 0:YZ] = big
        grid_ref[i, 0:USED, YZ : 2 * YZ] = big
        grid_ref[i, USED : 2 * USED, 0:YZ] = rest
        grid_ref[i, USED : 2 * USED, YZ : 2 * YZ] = rest

    bias_part = sum(slice_tile(t) for t in range(tiles))

    head = jnp.dot(
        half_ref[...], feat_t_ref[...], preferred_element_type=jnp.float32
    )
    bias_sum = jnp.sum(bias_part, axis=1, keepdims=True)
    on_row = lax.broadcasted_iota(jnp.int32, (8, head.shape[1]), 0)
    on_lane = lax.broadcasted_iota(jnp.int32, (8, head.shape[1]), 1)
    bias_row = jnp.sum(
        jnp.where(on_row == on_lane, bias_sum, 0.0), axis=0, keepdims=True
    )
    stat_ref[0:1, :] = jnp.concatenate([head[0:1], head[1:2]], axis=1)
    stat_ref[1:2, :] = jnp.concatenate([head[2:3], bias_row], axis=1)
    own_stat = pltpu.make_async_copy(stat_ref, h1_recv.at[my_dev], head_sems.at[1])
    own_stat.start()
    for dev in head_devs:
        head_copy(dev).start()
    reduce_three()

    def feature_tile(t):
        px = pl.ds(pl.multiple_of(t * TILE, TILE), TILE)
        fgrad_ref[:, px] = jnp.dot(
            weight_cols, half_ref[:, px], preferred_element_type=jnp.float32
        ).astype(jnp.bfloat16)

    run(feature_tile, FEATURE_UNROLL)
    plane_arrive(3, r3_recv)
    for q in range(planes):
        for s in range(OWN_MOST):
            owned_ref[:, s, q * YZ : (q + 1) * YZ] = r3_recv[q, s] + tv_ref[q, s]
    for q in plane_q:
        plane_copy(0, q, g1_send.at[q], g1_recv.at[my_q]).wait_send()
        plane_copy(1, q, g3_send.at[0], g3_recv.at[my_q]).wait_send()
        plane_copy(2, q, r1_send.at[q], r1_recv.at[my_q]).wait_send()
        plane_copy(3, q, r3_send.at[q], r3_recv.at[my_q]).wait_send()
    for g in line_g:
        line_copy(0, g, g2_send.at[g // 2], g2_recv.at[my_g]).wait_send()
        line_copy(1, g, r2_send, r2_recv.at[my_g]).wait_send()

    pltpu.make_async_copy(h1_recv, h1_recv, head_sems.at[1]).wait()
    count = h1_recv.shape[0]
    sums = [
        jnp.sum(h1_recv[n : n + count // 8], axis=0) for n in range(0, count, count // 8)
    ]
    while len(sums) > 1:
        sums = [a + b for a, b in zip(sums[::2], sums[1::2])]
    head_ref[...] = sums[0]
    sent = h1_recv.at[pl.ds(0, len(head_devs))]
    pltpu.make_async_copy(sent, sent, head_sems.at[0]).wait()


def finish(
    owned_in,
    stat_in,
    fgrad_in,
    owned_out,
    head_out,
    bias_out,
    fgrad_out,
    head_ref,
    bias_ref,
    sems,
):
    parts = 4
    rows = fgrad_in.shape[0] // parts
    copies = [
        (fgrad_in.at[pl.ds(n * rows, rows)], fgrad_out.at[pl.ds(n * rows, rows)])
        for n in range(parts)
    ]
    copies += [(owned_in, owned_out), (head_ref, head_out), (bias_ref, bias_out)]
    copies = [
        pltpu.make_async_copy(src, dst, sems.at[n])
        for n, (src, dst) in enumerate(copies)
    ]
    for copy in copies[:-2]:
        copy.start()
    width = head_ref.shape[1]
    head_ref[0:1, :] = stat_in[0:1, 0:width]
    head_ref[1:2, :] = stat_in[0:1, width : 2 * width]
    head_ref[2:3, :] = stat_in[1:2, 0:width]
    bias_ref[...] = stat_in[1, width : width + bias_ref.shape[0]]
    for copy in copies[-2:]:
        copy.start()
    for copy in copies:
        copy.wait()


def shards(side, rows_x, ids, table, tile_image, cell, frac, feat, weight, bias, cot):
    pixels = cell.shape[0]
    tiles = pixels // TILE
    planes = side * side
    groups = rows_x * 2
    images = ids.shape[0]
    f32, bf16, i32 = jnp.float32, jnp.bfloat16, jnp.int32
    chunk = (COEF, YZ)
    vmem = pl.BlockSpec(memory_space=pltpu.VMEM)
    hbm = pl.BlockSpec(memory_space=pltpu.HBM)
    table_rows = jnp.transpose(table, (1, 0, 2)).reshape(-1, CELLS)
    cell_rows = cell.reshape(pixels // 128, 128)
    owned, stat, fgrad = pl.pallas_call(
        functools.partial(kernel, side, rows_x),
        out_shape=(
            jax.ShapeDtypeStruct((COEF, OWN_MOST, CELLS), f32),
            jax.ShapeDtypeStruct((2, 128), f32),
            jax.ShapeDtypeStruct(feat.shape, bf16),
        ),
        in_specs=[hbm] * 9,
        out_specs=(vmem, vmem, vmem),
        scratch_shapes=[
            pltpu.SMEM(ids.shape, i32),
            pltpu.SMEM(tile_image.shape, i32),
            pltpu.SMEM(bias.shape, f32),
            pltpu.VMEM((planes, table_rows.shape[0] * 16 // COEF, YZ), f32),
            pltpu.VMEM(cell_rows.shape, i32),
            pltpu.VMEM(frac.shape, f32),
            pltpu.VMEM(feat.shape, bf16),
            pltpu.VMEM(weight.shape, bf16),
            pltpu.VMEM(cot.shape, bf16),
            pltpu.SemaphoreType.DMA((8 + planes,)),
            pltpu.VMEM((tiles, 2 * YZ, TILE), bf16),
            pltpu.VMEM((tiles, 3 * GX, TILE), f32),
            pltpu.VMEM((tiles, 8, TILE), f32),
            pltpu.VMEM((16, pixels), bf16),
            pltpu.VMEM((pixels, feat.shape[0]), bf16),
            pltpu.VMEM((IMG_ROW, ROWS, YZ), f32),
            pltpu.VMEM((2, ROWS, YZ), f32),
            pltpu.VMEM((2, 16 * GX, YZ), f32),
            pltpu.VMEM((IMG_ROW, 16 * GX, YZ), f32),
            pltpu.VMEM((IMG_ROW, 2 * USED, 2 * YZ), bf16),
            pltpu.VMEM((planes, OWN_MOST) + chunk, f32),
            pltpu.VMEM((2, 128), f32),
            pltpu.SMEM((images,), i32),
            pltpu.SMEM((images,), i32),
            pltpu.SMEM((images,), i32),
            pltpu.SMEM((planes * OWN_MOST,), i32),
            pltpu.VMEM((planes + 1, OWN_MOST * 9, YZ), f32),
            pltpu.VMEM((planes + 1, OWN_MOST * 9, YZ), f32),
            pltpu.VMEM((rows_x + 1, IMG_ROW * 9, YZ), f32),
            pltpu.VMEM((groups + 1, IMG_ROW * 9, YZ), f32),
            pltpu.VMEM((2, IMG_ROW * 9, YZ), f32),
            pltpu.VMEM((planes + 1, IMG_ROW * 9, YZ), f32),
            pltpu.VMEM((planes + 1, 2 * COEF, YZ), f32),
            pltpu.VMEM((planes + 1, 2 * COEF, YZ), f32),
            pltpu.VMEM((2,) + chunk, f32),
            pltpu.VMEM((groups + 1, 2) + chunk, f32),
            pltpu.VMEM((planes, OWN_MOST) + chunk, f32),
            pltpu.VMEM((planes, OWN_MOST) + chunk, f32),
            pltpu.VMEM((planes * groups, 2, 128), f32),
            pltpu.SemaphoreType.DMA((2,)),
            pltpu.SemaphoreType.DMA((2,)),
            pltpu.SemaphoreType.DMA((4, planes)),
            pltpu.SemaphoreType.DMA((4, planes)),
            pltpu.SemaphoreType.DMA((2, groups)),
            pltpu.SemaphoreType.DMA((2, groups)),
        ],
        compiler_params=pltpu.CompilerParams(
            collective_id=0, has_side_effects=True, vmem_limit_bytes=VMEM_LIMIT
        ),
    )(
        *(
            pltpu.with_memory_space_constraint(operand, pltpu.HBM)
            for operand in (
                ids,
                tile_image,
                bias,
                table_rows,
                cell_rows,
                frac,
                feat,
                weight,
                cot,
            )
        )
    )
    owned, head, bias_grad, fgrad = pl.pallas_call(
        finish,
        out_shape=(
            jax.ShapeDtypeStruct((COEF, OWN_MOST, CELLS), f32),
            jax.ShapeDtypeStruct(weight.shape, f32),
            jax.ShapeDtypeStruct(bias.shape, f32),
            jax.ShapeDtypeStruct(feat.shape, bf16),
        ),
        in_specs=[vmem, vmem, vmem],
        out_specs=(hbm, hbm, hbm, hbm),
        scratch_shapes=[
            pltpu.VMEM(weight.shape, f32),
            pltpu.VMEM(bias.shape, f32),
            pltpu.SemaphoreType.DMA((7,)),
        ],
        compiler_params=pltpu.CompilerParams(vmem_limit_bytes=16 << 20),
    )(owned, stat, fgrad)
    return jnp.transpose(owned, (1, 0, 2)), head, bias_grad, fgrad


def solution(mesh):
    rows_x = mesh.shape["img"]
    side = math.isqrt(mesh.shape["pix"] // 2)
    return jax.shard_map(
        functools.partial(shards, side, rows_x),
        mesh=mesh,
        in_specs=(
            P(),
            P(("img", "pix"), None, None),
            P(("img", "pix")),
            P(("img", "pix")),
            P(None, ("img", "pix")),
            P(None, ("img", "pix")),
            P(),
            P(),
            P(None, ("img", "pix")),
        ),
        out_specs=(P(("img", "pix"), None, None), P(), P(), P(None, ("img", "pix"))),
        check_vma=False,
    )
```
